256 devices in a mesh: dp: 32 (over x, z_lo, core), ctx: 8 (over z_hi, y).
Axes of the slice: x: 4, y: 4, z: 8 (z_hi: 2, z_lo: 4; z = z_hi * 4 + z_lo), core: 2. Of those that a mesh axis runs over, the one named last changes fastest.
Arguments:
- queries: bfloat16 [32768, 4096], P(('dp', 'ctx')), may hold values from -10 to 10
- keys: bfloat16 [32768, 4096], P(('dp', 'ctx')), may hold values from -10 to 10
- values: bfloat16 [32768, 4096], P(('dp', 'ctx')), may hold values from -6 to 6
- residual_in: bfloat16 [32768, 7168], P(('dp', 'ctx')), may hold values from -40 to 40
- out_weight: bfloat16 [4096, 7168], P('ctx', 'dp'), may hold values from -1.25 to 1.25
- norm_gain: float32 [7168], replicated, may hold values from 0.5 to 1.5
- norm_bias: float32 [7168], replicated, may hold values from -3 to 3
Outputs:
- layer_out: bfloat16 [32768, 7168], P(('dp', 'ctx'))
The draws below stay inside these ranges and needn't reach their ends.
All inputs are finite; a program needn't handle non-finite values.
Results may differ from the reference program's by a relative error of at most 0.0085.
Values may be sent and summed in bfloat16 or wider, within the bound.
No kernel may reach another device: no remote copies, remote signals or barrier semaphores. Data moves between devices by JAX's collectives and lax.ppermute only.
A program may use at most 128 MiB of HBM per device.

```python
import math
import jax
import jax.numpy as jnp
from jax import lax

D = 7168
HEADS = 32
HD = 128
SEQ = 1024
TOKENS = 32768
GROUP_HEADS = 4
N_DP = 32
N_CTX = 8


def base_field(key, shape):
    return jnp.clip(jax.random.normal(key, shape, jnp.float32), -4.0, 4.0)


def draw_queries(key, part):
    field = base_field(jax.random.fold_in(key, 1), (TOKENS, HEADS * HD))
    return field.astype(jnp.bfloat16)


def draw_keys(key, part):
    field = base_field(jax.random.fold_in(key, 2), (TOKENS, HEADS * HD))
    return field.astype(jnp.bfloat16)


def draw_residual_in(key, part):
    field = base_field(jax.random.fold_in(key, 3), (TOKENS, D))
    lower, upper = (0.3, 3.0)
    row_scale = jnp.exp(jax.random.uniform(jax.random.fold_in(key, 4), (TOKENS, 1), jnp.float32, math.log(lower), math.log(upper)))
    col_scale = jnp.exp(jax.random.uniform(jax.random.fold_in(key, 5), (1, D), jnp.float32, math.log(lower), math.log(upper)))
    return (field * row_scale * col_scale).astype(jnp.bfloat16)


def levels(stream_key, shape, shards, smallest, top_value):
    level = 1.0
    for axis_at, blocks in shards:
        heights = jax.random.uniform(jax.random.fold_in(jax.random.fold_in(stream_key, 6), axis_at), (blocks,), jnp.float32, smallest / len(shards), top_value / len(shards))
        level = level * jnp.repeat(jnp.exp(heights), shape[axis_at] // blocks).reshape((-1,) + (1,) * (len(shape) - 1 - axis_at))
    return level


def bell_draw(key, dims, deviation, reach, cuts=(), held_as=jnp.bfloat16):
    result = deviation * jax.random.normal(key, dims, jnp.float32)
    if cuts:
        result = result * levels(key, dims, cuts, -0.22, 0.18)
    return jnp.clip(result, -reach, reach).astype(held_as)


def setup_inputs(seed: int = 0) -> dict:
    arg_keys = jax.random.split(jax.random.key(seed), 8)
    return {
        "queries": draw_queries(jax.random.fold_in(arg_keys[7], 71), 0),
        "keys": draw_keys(jax.random.fold_in(arg_keys[7], 71), 0),
        "values": bell_draw(arg_keys[2], (TOKENS, HEADS * HD), 1.0, 6.0, ((0, 256),)),
        "residual_in": draw_residual_in(jax.random.fold_in(arg_keys[7], 71), 0),
        "out_weight": bell_draw(arg_keys[4], (HEADS * HD, D), 0.08, 1.25, ((0, 8), (1, 32))),
        "norm_gain": jnp.clip(jax.random.uniform(arg_keys[5], (D,), jnp.float32, 0.5, 1.5), 0.5, 1.5),
        "norm_bias": bell_draw(arg_keys[6], (D,), 0.5, 3.0, (), jnp.float32),
    }


deepnorm_alpha = 96.0 ** 0.25
norm_eps = 1e-05

def attend(queries, keys, values):
    scale = 1.0 / math.sqrt(HD)
    scores = jnp.einsum('qhd,khd->hqk', queries.astype(jnp.float32), keys.astype(jnp.float32)) * scale
    position = jnp.arange(SEQ)
    causal = position[:, None] >= position[None, :]
    scores = jnp.where(causal[None], scores, -1e+30)
    highest = lax.optimization_barrier(jnp.max(scores, axis=-1, keepdims=True))
    expo = jnp.exp(scores - highest)
    probs = (expo / lax.optimization_barrier(jnp.sum(expo, axis=-1, keepdims=True))).astype(jnp.bfloat16)
    heads_out = jnp.einsum('hqk,khd->qhd', probs.astype(jnp.float32), values.astype(jnp.float32))
    return heads_out.astype(jnp.bfloat16).reshape(SEQ, HEADS * HD)

def reference(queries, keys, values, residual_in, out_weight, norm_gain, norm_bias):
    weight = out_weight.reshape(N_CTX, GROUP_HEADS * HD, D).astype(jnp.float32)

    def one_sequence(inputs):
        seq_q, seq_k, seq_v, seq_x = inputs
        heads_out = attend(seq_q.reshape(SEQ, HEADS, HD), seq_k.reshape(SEQ, HEADS, HD), seq_v.reshape(SEQ, HEADS, HD))
        grouped = heads_out.reshape(SEQ, N_CTX, GROUP_HEADS * HD).astype(jnp.float32)
        group_part = jnp.einsum('sgw,gwd->gsd', grouped, weight)
        group_part = lax.optimization_barrier(group_part.astype(jnp.bfloat16)).astype(jnp.float32)
        attn_out = lax.optimization_barrier(lax.optimization_barrier(jnp.sum(group_part, axis=0)).astype(jnp.bfloat16)).astype(jnp.float32)
        mixed = deepnorm_alpha * seq_x.astype(jnp.float32) + attn_out
        mean = lax.optimization_barrier(jnp.mean(mixed, axis=-1, keepdims=True))
        centered = mixed - mean
        var = lax.optimization_barrier(jnp.mean(centered * centered, axis=-1, keepdims=True))
        normed = centered * lax.rsqrt(var + norm_eps) * norm_gain + norm_bias
        return normed.astype(jnp.bfloat16)
    stacked = (queries.reshape(N_DP, SEQ, HEADS * HD), keys.reshape(N_DP, SEQ, HEADS * HD), values.reshape(N_DP, SEQ, HEADS * HD), residual_in.reshape(N_DP, SEQ, D))
    layer_out = lax.map(one_sequence, stacked)
    return layer_out.reshape(TOKENS, D)
```

```python
import functools
import math

import jax
import jax.numpy as jnp
from jax import lax
from jax.experimental import pallas as pl
from jax.experimental.pallas import tpu as pltpu
from jax.sharding import Mesh, PartitionSpec as P

HD = 128
GROUP = 512
ROWS = 128
SEQ_HALF = 512
D = 7168
HALF = D // 2

deepnorm_alpha = 96.0**0.25
norm_eps = 1e-05
score_scale = math.log2(math.e) / math.sqrt(HD)

AXES = ("x", "zl", "c", "zh", "y")


def ring(n, step):
    return [(i, (i + step) % n) for i in range(n)]


def z_ring(step):
    pairs = []
    for z in range(8):
        to = (z + step) % 8
        pairs.append(((z % 4) * 2 + z // 4, (to % 4) * 2 + to // 4))
    return pairs


def spread_pairs():
    pairs = []
    for dp in range(32):
        core, x, zl = dp // 16, dp // 4 % 4, dp % 4
        pairs.append((dp, x * 8 + zl * 2 + core))
    return pairs


def attention_kernel(causal, where_ref, *refs):
    q_refs, k_refs, v_refs = refs[0:4], refs[4:8], refs[8:12]
    o_ref, lse_ref = refs[12], refs[13]
    head = pl.program_id(0)
    y = where_ref[0]
    zh = where_ref[1]

    def work():
        q = jnp.concatenate([r[...] for r in q_refs], axis=0)
        k = jnp.concatenate([r[...] for r in k_refs], axis=0)
        v = jnp.concatenate([r[...] for r in v_refs], axis=0)
        scores = lax.dot_general(k, q, (((1,), (1,)), ((), ())), preferred_element_type=jnp.float32)
        if causal:
            def position(axis):
                at = lax.broadcasted_iota(jnp.int32, scores.shape, axis)
                return ((y - at // ROWS) & 3) * ROWS + (at & (ROWS - 1))
            scores = jnp.where(position(0) <= position(1), scores, -1e30)
        highest = jnp.max(scores, axis=0, keepdims=True)
        expo = jnp.exp2((scores - highest) * score_scale)
        total = jnp.sum(expo, axis=0, keepdims=True)
        out = lax.dot_general(
            v, expo.astype(jnp.bfloat16), (((0,), (0,)), ((), ())), preferred_element_type=jnp.float32
        )
        o_ref[...] = (out / total).astype(jnp.bfloat16)
        lse_ref[pl.ds(head, 1), :] = highest * score_scale + jnp.log2(total)

    if causal:
        work()
    else:
        pl.when(zh == 0)(work)


def attention(causal, where, q, k, v):
    spec = pl.BlockSpec((ROWS, HD), lambda h, w: (0, h))
    heads = GROUP // HD
    return pl.pallas_call(
        functools.partial(attention_kernel, causal),
        grid_spec=pltpu.PrefetchScalarGridSpec(
            num_scalar_prefetch=1,
            grid=(heads,),
            in_specs=[spec] * 12,
            out_specs=[
                pl.BlockSpec((HD, SEQ_HALF), lambda h, w: (h, 0)),
                pl.BlockSpec((8, SEQ_HALF), lambda h, w: (0, 0)),
            ],
        ),
        out_shape=[
            jax.ShapeDtypeStruct((GROUP, SEQ_HALF), jnp.bfloat16),
            jax.ShapeDtypeStruct((8, SEQ_HALF), jnp.float32),
        ],
        compiler_params=pltpu.CompilerParams(vmem_limit_bytes=24 * 1024 * 1024),
        cost_estimate=pl.CostEstimate(
            flops=heads * 4 * SEQ_HALF * SEQ_HALF * HD, bytes_accessed=2 * 1024 * 1024,
            transcendentals=heads * SEQ_HALF * SEQ_HALF),
        name="attend_causal" if causal else "attend_cross",
    )(where, *q, *k, *v)


def merge_kernel(where_ref, own_ref, far_ref, own_lse_ref, far_lse_ref, out_ref):
    head = pl.program_id(0)
    own_lse = own_lse_ref[pl.ds(head, 1), :]
    far_lse = jnp.where(where_ref[1] == 1, far_lse_ref[pl.ds(head, 1), :], -1e30)
    highest = jnp.maximum(own_lse, far_lse)
    own_part = jnp.exp2(own_lse - highest)
    far_part = jnp.exp2(far_lse - highest)
    total = own_part + far_part
    mixed = own_ref[...].astype(jnp.float32) * (own_part / total)
    mixed = mixed + far_ref[...].astype(jnp.float32) * (far_part / total)
    out_ref[...] = mixed.T.astype(jnp.bfloat16)


def merge(where, own, far, own_lse, far_lse):
    block = pl.BlockSpec((HD, SEQ_HALF), lambda h, w: (h, 0))
    stat = pl.BlockSpec((8, SEQ_HALF), lambda h, w: (0, 0))
    return pl.pallas_call(
        merge_kernel,
        grid_spec=pltpu.PrefetchScalarGridSpec(
            num_scalar_prefetch=1,
            grid=(GROUP // HD,),
            in_specs=[block, block, stat, stat],
            out_specs=pl.BlockSpec((SEQ_HALF, HD), lambda h, w: (0, h)),
        ),
        out_shape=jax.ShapeDtypeStruct((SEQ_HALF, GROUP), jnp.bfloat16),
        compiler_params=pltpu.CompilerParams(vmem_limit_bytes=16 * 1024 * 1024),
        cost_estimate=pl.CostEstimate(flops=4 * 512 * 512, bytes_accessed=3 * 512 * 1024, transcendentals=0),
        name="merge_halves",
    )(where, own, far, own_lse, far_lse)


def norm_kernel(where_ref, own_ref, peer_ref, res_ref, gain_ref, bias_ref, out_ref):
    core = where_ref[2]
    mine = pl.ds(pl.multiple_of(core * HALF, HALF), HALF)
    other = pl.ds(pl.multiple_of((1 - core) * HALF, HALF), HALF)
    a = deepnorm_alpha * res_ref[:, mine].astype(jnp.float32) + own_ref[...].astype(jnp.float32)
    b = deepnorm_alpha * res_ref[:, other].astype(jnp.float32) + peer_ref[...].astype(jnp.float32)
    mean = (jnp.sum(a, -1, keepdims=True) + jnp.sum(b, -1, keepdims=True)) / D
    a = a - mean
    b = b - mean
    var = (jnp.sum(a * a, -1, keepdims=True) + jnp.sum(b * b, -1, keepdims=True)) / D
    inv = lax.rsqrt(var + norm_eps)
    out_ref[:, mine] = (a * inv * gain_ref[:, mine] + bias_ref[:, mine]).astype(jnp.bfloat16)
    out_ref[:, other] = (b * inv * gain_ref[:, other] + bias_ref[:, other]).astype(jnp.bfloat16)


def layer_norm(where, own, peer, residual, gain, bias):
    rows = 32
    half = pl.BlockSpec((rows, HALF), lambda i, w: (i, 0))
    full = pl.BlockSpec((rows, D), lambda i, w: (i, 0))
    vector = pl.BlockSpec((1, D), lambda i, w: (0, 0))
    return pl.pallas_call(
        norm_kernel,
        grid_spec=pltpu.PrefetchScalarGridSpec(
            num_scalar_prefetch=1,
            grid=(ROWS // rows,),
            in_specs=[half, half, full, vector, vector],
            out_specs=full,
        ),
        out_shape=jax.ShapeDtypeStruct((ROWS, D), jnp.bfloat16),
        compiler_params=pltpu.CompilerParams(vmem_limit_bytes=24 * 1024 * 1024),
        cost_estimate=pl.CostEstimate(flops=10 * ROWS * D, bytes_accessed=6 * ROWS * D, transcendentals=0),
        name="layer_norm",
    )(where, own, peer, residual, gain.reshape(1, D), bias.reshape(1, D))


def exchange_y(block, y, only_low=False):
    width = block.shape[1] // 4
    parts = []
    for step in range(4):
        to = (y + step) & 3
        part = lax.dynamic_slice_in_dim(block, to * width, width, axis=1)
        if step:
            if only_low:
                pairs = [(i, (i + step) % 4) for i in range(4)]
                part = lax.ppermute(part, ("zh", "y"), pairs)
            else:
                part = lax.ppermute(part, "y", ring(4, step))
        parts.append(part)
    return parts


def gather_weight(weight):
    shard = lax.ppermute(weight.T, ("x", "zl", "c"), spread_pairs())
    z = lax.axis_index("zh") * 4 + lax.axis_index("zl")
    column = jnp.zeros((2, 4, 224, 512), jnp.bfloat16)

    def put(column, part, at):
        return lax.dynamic_update_slice(column, part[None, None], ((at >> 2) & 1, at & 3, 0, 0))

    column = put(column, shard, z)
    up = down = shard
    for step in range(1, 5):
        up = lax.ppermute(up, ("zl", "zh"), z_ring(1))
        column = put(column, up, (z - step) & 7)
        if step < 4:
            down = lax.ppermute(down, ("zl", "zh"), z_ring(-1))
            column = put(column, down, (z + step) & 7)
    column = jnp.concatenate([column[0].reshape(896, 512), column[1].reshape(896, 512)], axis=1)
    left = lax.ppermute(column, "x", ring(4, 1))
    right = lax.ppermute(column, "x", ring(4, -1))
    far = jnp.concatenate(
        [lax.ppermute(left[:448], "x", ring(4, 1)), lax.ppermute(right[448:], "x", ring(4, -1))], axis=0
    )
    x = lax.axis_index("x")
    whole = jnp.zeros((4, 896, 1024), jnp.bfloat16)
    for part, at in ((column, x), (left, x - 1), (right, x + 1), (far, x + 2)):
        whole = lax.dynamic_update_slice(whole, part[None], (at & 3, 0, 0))
    return whole.reshape(HALF, 1024)


def local(queries, keys, values, residual_in, out_weight, norm_gain, norm_bias):
    y = lax.axis_index("y")
    zh = lax.axis_index("zh")
    core = lax.axis_index("c")
    where = jnp.stack([y, zh, core]).astype(jnp.int32)

    weight = gather_weight(out_weight)

    outs = []
    peers = []
    for chunk in range(2):
        cut = slice(chunk * 2048, chunk * 2048 + 2048)
        far_q = lax.ppermute(queries[:, cut], "zh", [(1, 0)])
        k = exchange_y(keys[:, cut], y)
        v = exchange_y(values[:, cut], y)
        q = exchange_y(queries[:, cut], y)
        far_q = exchange_y(far_q, y, True)
        far_out, far_lse = attention(False, where, far_q, k, v)
        far_out = lax.ppermute(far_out, "zh", [(0, 1)])
        far_lse = lax.ppermute(far_lse, "zh", [(0, 1)])
        own_out, own_lse = attention(True, where, q, k, v)
        out = merge(where, own_out, far_out, own_lse, far_lse)
        outs.append(out)
        peers.append(lax.ppermute(out, "c", ring(2, 1)))
    heads = jnp.concatenate(
        [jnp.concatenate(outs, 1).reshape(4, ROWS, 1024), jnp.concatenate(peers, 1).reshape(4, ROWS, 1024)], axis=1
    )

    cut = HALF // 2
    low, high = weight[:cut], weight[cut:]

    def project(step, part):
        return lax.dot_general(
            heads[step], part, (((1,), (1,)), ((), ())), preferred_element_type=jnp.float32
        )

    def send(block, step):
        return lax.ppermute(block.astype(jnp.bfloat16), "y", ring(4, step))

    up_1 = send(project(2, low), 1)
    down_1 = send(project(2, high), -1)
    up_2 = send(project(3, high), 1)
    down_2 = send(project(1, low), -1)
    up_3 = send(project(3, low) + up_1.astype(jnp.float32), 1)
    down_3 = send(project(1, high) + down_1.astype(jnp.float32), -1)
    total_low = project(0, low) + down_2.astype(jnp.float32) + up_3.astype(jnp.float32)
    total_high = project(0, high) + up_2.astype(jnp.float32) + down_3.astype(jnp.float32)
    total = jnp.concatenate([total_low.astype(jnp.bfloat16), total_high.astype(jnp.bfloat16)], axis=1)
    peer = lax.ppermute(total[ROWS:], "c", ring(2, 1))
    return layer_norm(where, total[:ROWS], peer, residual_in, norm_gain, norm_bias)


def solution(mesh):
    fine = Mesh(mesh.devices.reshape(4, 4, 2, 2, 4), AXES)
    tokens = P(AXES, None)
    in_specs = (tokens, tokens, tokens, tokens, P(("zh", "y"), ("x", "zl", "c")), P(), P())
    return jax.shard_map(local, mesh=fine, in_specs=in_specs, out_specs=tokens, check_vma=False)
```

```python
import functools
import math

import jax
import jax.numpy as jnp
from jax import lax
from jax.experimental import pallas as pl
from jax.experimental.pallas import tpu as pltpu
from jax.sharding import Mesh, PartitionSpec as P

HD = 128
GROUP = 512
ROWS = 128
SEQ_HALF = 512
D = 7168
HALF = D // 2

deepnorm_alpha = 96.0**0.25
norm_eps = 1e-05
score_scale = math.log2(math.e) / math.sqrt(HD)

AXES = ("x", "zl", "c", "zh", "y")


def ring(n, step):
    return [(i, (i + step) % n) for i in range(n)]


def spread_pairs(flip):
    pairs = []
    for s in range(32):
        half = (s // 8 % 2) ^ flip
        place = s % 8 * 2 + half
        pairs.append((s, (place % 4) * 8 + (place // 4) * 2 + s // 16))
    return pairs


def softmax_part(q, k, v, keep):
    scores = lax.dot_general(k, q, (((1,), (1,)), ((), ())), preferred_element_type=jnp.float32)
    if keep is not None:
        scores = jnp.where(keep, scores, -1e30)
    highest = jnp.max(scores, axis=0, keepdims=True)
    expo = jnp.exp2((scores - highest) * score_scale)
    total = jnp.sum(expo, axis=0, keepdims=True)
    out = lax.dot_general(
        v, expo.astype(jnp.bfloat16), (((0,), (0,)), ((), ())), preferred_element_type=jnp.float32
    )
    return (out / total).astype(jnp.bfloat16), highest * score_scale + jnp.log2(total)


def own_kernel(where_ref, *refs):
    q_refs, k_refs, v_refs, o_ref, lse_ref = refs[0:4], refs[4:8], refs[8:12], refs[12], refs[13]
    head = pl.program_id(0)
    y = where_ref[0]
    q, k, v = (jnp.concatenate([r[...] for r in part], axis=0) for part in (q_refs, k_refs, v_refs))

    def position(axis):
        at = lax.broadcasted_iota(jnp.int32, (SEQ_HALF, SEQ_HALF), axis)
        return ((y - at // ROWS) & 3) * ROWS + (at & (ROWS - 1))

    out, lse = softmax_part(q, k, v, position(0) <= position(1))
    o_ref[...] = out
    lse_ref[pl.ds(head, 1), :] = lse


def far_kernel(where_ref, q_ref, *refs):
    k_refs, v_refs, o_ref, lse_ref = refs[0:4], refs[4:8], refs[8], refs[9]
    head = pl.program_id(0)

    @pl.when(where_ref[1] == 0)
    def _():
        k, v = (jnp.concatenate([r[...] for r in part], axis=0) for part in (k_refs, v_refs))
        out, lse = softmax_part(q_ref[...], k, v, None)
        o_ref[pl.ds(pl.multiple_of(head * HD, HD), HD), :] = out
        lse_ref[pl.ds(head, 1), :] = lse

        @pl.when(head == GROUP // HD - 1)
        def _():
            rest = lse_ref[0:4, :]
            terms = []
            for _ in range(3):
                term = rest.astype(jnp.bfloat16).astype(jnp.float32)
                terms.append(term)
                rest = rest - term
            terms.append(jnp.zeros_like(rest))
            o_ref[pl.ds(GROUP, 16), :] = jnp.concatenate(terms, axis=0).astype(jnp.bfloat16)


def attention_cost(heads):
    return pl.CostEstimate(
        flops=heads * 4 * SEQ_HALF * SEQ_HALF * HD, bytes_accessed=2 * 1024 * 1024,
        transcendentals=heads * SEQ_HALF * SEQ_HALF)


def attend_own(where, chunk, q, kv):
    heads = GROUP // HD
    q_spec = pl.BlockSpec((ROWS, HD), lambda h, w: (0, heads * chunk + h))
    k_spec = pl.BlockSpec((ROWS, HD), lambda h, w: (0, h))
    v_spec = pl.BlockSpec((ROWS, HD), lambda h, w: (0, heads + h))
    return pl.pallas_call(
        own_kernel,
        grid_spec=pltpu.PrefetchScalarGridSpec(
            num_scalar_prefetch=1,
            grid=(heads,),
            in_specs=[q_spec] * 4 + [k_spec] * 4 + [v_spec] * 4,
            out_specs=[
                pl.BlockSpec((HD, SEQ_HALF), lambda h, w: (h, 0)),
                pl.BlockSpec((8, SEQ_HALF), lambda h, w: (0, 0)),
            ],
        ),
        out_shape=[
            jax.ShapeDtypeStruct((GROUP, SEQ_HALF), jnp.bfloat16),
            jax.ShapeDtypeStruct((8, SEQ_HALF), jnp.float32),
        ],
        compiler_params=pltpu.CompilerParams(vmem_limit_bytes=24 * 1024 * 1024),
        cost_estimate=attention_cost(heads),
        name="attend_own",
    )(where, *q, *kv, *kv)


def attend_far(where, q, kv):
    heads = GROUP // HD
    q_spec = pl.BlockSpec((SEQ_HALF, HD), lambda h, w: (0, h))
    k_spec = pl.BlockSpec((ROWS, HD), lambda h, w: (0, h))
    v_spec = pl.BlockSpec((ROWS, HD), lambda h, w: (0, heads + h))
    return pl.pallas_call(
        far_kernel,
        grid_spec=pltpu.PrefetchScalarGridSpec(
            num_scalar_prefetch=1,
            grid=(heads,),
            in_specs=[q_spec] + [k_spec] * 4 + [v_spec] * 4,
            out_specs=pl.BlockSpec((GROUP + 16, SEQ_HALF), lambda h, w: (0, 0)),
            scratch_shapes=[pltpu.VMEM((8, SEQ_HALF), jnp.float32)],
        ),
        out_shape=jax.ShapeDtypeStruct((GROUP + 16, SEQ_HALF), jnp.bfloat16),
        compiler_params=pltpu.CompilerParams(vmem_limit_bytes=24 * 1024 * 1024),
        cost_estimate=attention_cost(heads),
        name="attend_far",
    )(where, q, *kv, *kv)


def merge_kernel(where_ref, own_ref, far_ref, own_lse_ref, out_ref):
    terms = far_ref[pl.ds(GROUP, 16), :].astype(jnp.float32)
    far_lse = terms[0:4] + terms[4:8] + terms[8:12]
    far_lse = jnp.where(where_ref[1] == 1, far_lse, -1e30)
    own_lse = own_lse_ref[0:4, :]
    highest = jnp.maximum(own_lse, far_lse)
    own_part = jnp.exp2(own_lse - highest)
    far_part = jnp.exp2(far_lse - highest)
    total = own_part + far_part
    own_part = own_part / total
    far_part = far_part / total
    for head in range(GROUP // HD):
        rows = pl.ds(head * HD, HD)
        mixed = own_ref[rows, :].astype(jnp.float32) * own_part[head : head + 1]
        mixed = mixed + far_ref[rows, :].astype(jnp.float32) * far_part[head : head + 1]
        out_ref[:, rows] = mixed.T.astype(jnp.bfloat16)


def merge(where, own, far, own_lse):
    whole = pl.BlockSpec(memory_space=pltpu.VMEM)
    return pl.pallas_call(
        merge_kernel,
        in_specs=[pl.BlockSpec(memory_space=pltpu.SMEM), whole, whole, whole],
        out_specs=whole,
        out_shape=jax.ShapeDtypeStruct((SEQ_HALF, GROUP), jnp.bfloat16),
        compiler_params=pltpu.CompilerParams(vmem_limit_bytes=16 * 1024 * 1024),
        cost_estimate=pl.CostEstimate(flops=4 * 512 * 512, bytes_accessed=3 * 512 * 1024, transcendentals=0),
        name="merge_halves",
    )(where, own, far, own_lse)


def norm_kernel(where_ref, own_0, own_1, peer_0, peer_1, res_ref, gain_ref, bias_ref, out_ref):
    core = where_ref[2]
    quarter = HALF // 2
    blocks = []
    for half, part, ref in ((core, 0, own_0), (core, 1, own_1), (1 - core, 0, peer_0), (1 - core, 1, peer_1)):
        at = pl.ds(pl.multiple_of(half * HALF + part * quarter, quarter), quarter)
        mixed = deepnorm_alpha * res_ref[:, at].astype(jnp.float32) + ref[...].astype(jnp.float32)
        blocks.append((at, mixed))
    mean = sum(jnp.sum(b, -1, keepdims=True) for _, b in blocks) / D
    blocks = [(at, b - mean) for at, b in blocks]
    var = sum(jnp.sum(b * b, -1, keepdims=True) for _, b in blocks) / D
    inv = lax.rsqrt(var + norm_eps)
    for at, b in blocks:
        out_ref[:, at] = (b * inv * gain_ref[:, at] + bias_ref[:, at]).astype(jnp.bfloat16)


def layer_norm(where, own, peer, residual, gain, bias):
    rows = 32
    part = pl.BlockSpec((rows, HALF // 2), lambda i, w: (i, 0))
    full = pl.BlockSpec((rows, D), lambda i, w: (i, 0))
    vector = pl.BlockSpec((1, D), lambda i, w: (0, 0))
    return pl.pallas_call(
        norm_kernel,
        grid_spec=pltpu.PrefetchScalarGridSpec(
            num_scalar_prefetch=1,
            grid=(ROWS // rows,),
            in_specs=[part] * 4 + [full, vector, vector],
            out_specs=full,
        ),
        out_shape=jax.ShapeDtypeStruct((ROWS, D), jnp.bfloat16),
        compiler_params=pltpu.CompilerParams(vmem_limit_bytes=24 * 1024 * 1024),
        cost_estimate=pl.CostEstimate(flops=10 * ROWS * D, bytes_accessed=6 * ROWS * D, transcendentals=0),
        name="layer_norm",
    )(where, *own, *peer, residual, gain.reshape(1, D), bias.reshape(1, D))


def after(value, *others):
    return lax.optimization_barrier((value, *others))[0]


def exchange_y(arrays, y, starts):
    parts = []
    for step in range(4):
        at = ((y + step) & 3) * GROUP
        part = jnp.concatenate(
            [lax.dynamic_slice_in_dim(a, s + at, GROUP, axis=1) for a, s in zip(arrays, starts)], axis=1
        )
        parts.append(part)
    return [parts[0]] + [lax.ppermute(parts[s], "y", ring(4, s)) for s in (1, 2, 3)]


def gather_weight(weight, s):
    late = (s >> 3) & 1 == 1
    low, high = weight.T[:112], weight.T[112:]
    first = lax.ppermute(jnp.where(late, high, low), ("x", "zl", "c"), spread_pairs(0))
    second = lax.ppermute(jnp.where(late, low, high), ("x", "zl", "c"), spread_pairs(1))
    odd = lax.axis_index("x") & 1 == 1
    part_0 = jnp.where(odd, second, first)
    part_1 = jnp.where(odd, first, second)
    return part_0, part_1


def whole_weight(part):
    return lax.all_gather(part, ("zh", "zl", "x"), axis=0, tiled=True).reshape(2, HALF // 2, GROUP)


def send(block, step):
    return lax.ppermute(block.astype(jnp.bfloat16), "y", ring(4, step))


def local(queries, keys, values, residual_in, out_weight, norm_gain, norm_bias):
    y = lax.axis_index("y")
    zh = lax.axis_index("zh")
    core = lax.axis_index("c")
    where = jnp.stack([y, zh, core]).astype(jnp.int32)
    shard = (lax.axis_index("x") * 4 + lax.axis_index("zl")) * 2 + core

    part_0, part_1 = gather_weight(out_weight, shard)
    weights = [whole_weight(part_0)]
    queries = after(queries, part_0)

    q = exchange_y([queries, queries], y, [0, 2048])
    q_0 = jnp.concatenate([b[:, :GROUP] for b in q], axis=0)
    q_1 = jnp.concatenate([b[:, GROUP:] for b in q], axis=0)
    far_q0 = lax.ppermute(q_0, "zh", [(1, 0)])
    keys, values, _ = lax.optimization_barrier((keys, values, q[2]))
    weights.append(whole_weight(after(part_1, q[2])))
    kv_0 = exchange_y([keys, values], y, [0, 0])
    far_q1 = lax.ppermute(after(q_1, far_q0), "zh", [(1, 0)])
    keys, values, _ = lax.optimization_barrier((keys, values, kv_0[2]))
    kv_1 = exchange_y([keys, values], y, [2048, 2048])

    outs = []
    peers = []
    for chunk, far_q, kv in ((0, far_q0, kv_0), (1, far_q1, kv_1)):
        far_out = attend_far(where, far_q, kv)
        far_out = lax.ppermute(far_out, "zh", [(0, 1)])
        own_out, own_lse = attend_own(where, chunk, q, kv)
        out = merge(where, own_out, far_out, own_lse)
        outs.append(out)
        peers.append(lax.ppermute(out, "c", ring(2, 1)))
    own = jnp.concatenate(outs, 1).reshape(4, ROWS, 2, GROUP)
    other = jnp.concatenate(peers, 1).reshape(4, ROWS, 2, GROUP)

    sums = []
    peer_sums = []
    for weight in weights:

        def project(heads, step):
            return lax.dot_general(
                heads[step], weight, (((1, 2), (0, 2)), ((), ())), preferred_element_type=jnp.float32
            )

        up_1 = send(project(own, 2), 1)
        down_1 = send(project(other, 2), -1)
        up_2 = send(project(other, 3), 1)
        down_2 = send(project(own, 1), -1)
        up_3 = send(project(own, 3) + up_1.astype(jnp.float32), 1)
        down_3 = send(project(other, 1) + down_1.astype(jnp.float32), -1)
        total_other = project(other, 0) + up_2.astype(jnp.float32) + down_3.astype(jnp.float32)
        peer_sums.append(lax.ppermute(total_other.astype(jnp.bfloat16), "c", ring(2, 1)))
        total_own = project(own, 0) + down_2.astype(jnp.float32) + up_3.astype(jnp.float32)
        sums.append(total_own.astype(jnp.bfloat16))
    return layer_norm(where, sums, peer_sums, residual_in, norm_gain, norm_bias)


def solution(mesh):
    fine = Mesh(mesh.devices.reshape(4, 4, 2, 2, 4), AXES)
    tokens = P(AXES, None)
    in_specs = (tokens, tokens, tokens, tokens, P(("zh", "y"), ("x", "zl", "c")), P(), P())
    return jax.shard_map(local, mesh=fine, in_specs=in_specs, out_specs=tokens, check_vma=False)
```

```python
import functools
import math

import jax
import jax.numpy as jnp
from jax import lax
from jax.experimental import pallas as pl
from jax.experimental.pallas import tpu as pltpu
from jax.sharding import Mesh, PartitionSpec as P

HD = 128
GROUP = 512
ROWS = 128
SEQ_HALF = 512
D = 7168
HALF = D // 2
BLOCK = HALF // 4

deepnorm_alpha = 96.0**0.25
norm_eps = 1e-05
score_scale = math.log2(math.e) / math.sqrt(HD)

AXES = ("x", "zl", "c", "zh", "y")


def ring(n, step):
    return [(i, (i + step) % n) for i in range(n)]


def spread_pairs():
    return [(s, (s // 4 % 4) * 8 + (s % 4) * 2 + s // 16) for s in range(32)]


def softmax_part(q, k, v, keep):
    scores = lax.dot_general(k, q, (((1,), (1,)), ((), ())), preferred_element_type=jnp.float32)
    if keep is not None:
        scores = jnp.where(keep, scores, -1e30)
    highest = jnp.max(scores, axis=0, keepdims=True)
    expo = jnp.exp2((scores - highest) * score_scale)
    total = jnp.sum(expo, axis=0, keepdims=True)
    out = lax.dot_general(
        v, expo.astype(jnp.bfloat16), (((0,), (0,)), ((), ())), preferred_element_type=jnp.float32
    )
    return (out / total).astype(jnp.bfloat16), highest * score_scale + jnp.log2(total)


def own_kernel(where_ref, *refs):
    q_refs, k_refs, v_refs, o_ref, lse_ref = refs[0:4], refs[4:8], refs[8:12], refs[12], refs[13]
    head = pl.program_id(0)
    y = where_ref[0]
    q, k, v = (jnp.concatenate([r[...] for r in part], axis=0) for part in (q_refs, k_refs, v_refs))

    def position(axis):
        at = lax.broadcasted_iota(jnp.int32, (SEQ_HALF, SEQ_HALF), axis)
        return ((y - at // ROWS) & 3) * ROWS + (at & (ROWS - 1))

    out, lse = softmax_part(q, k, v, position(0) <= position(1))
    o_ref[...] = out
    lse_ref[pl.ds(head, 1), :] = lse


def far_kernel(where_ref, q_ref, *refs):
    k_refs, v_refs, o_ref, lse_ref = refs[0:4], refs[4:8], refs[8], refs[9]
    head = pl.program_id(0)

    @pl.when(where_ref[1] == 0)
    def _():
        k, v = (jnp.concatenate([r[...] for r in part], axis=0) for part in (k_refs, v_refs))
        out, lse = softmax_part(q_ref[...], k, v, None)
        o_ref[pl.ds(pl.multiple_of(head * HD, HD), HD), :] = out
        lse_ref[pl.ds(head, 1), :] = lse

        @pl.when(head == GROUP // HD - 1)
        def _():
            rest = lse_ref[0:4, :]
            terms = []
            for _ in range(3):
                term = rest.astype(jnp.bfloat16).astype(jnp.float32)
                terms.append(term)
                rest = rest - term
            terms.append(jnp.zeros_like(rest))
            o_ref[pl.ds(GROUP, 16), :] = jnp.concatenate(terms, axis=0).astype(jnp.bfloat16)


def attention_cost(heads):
    return pl.CostEstimate(
        flops=heads * 4 * SEQ_HALF * SEQ_HALF * HD, bytes_accessed=2 * 1024 * 1024,
        transcendentals=heads * SEQ_HALF * SEQ_HALF)


def attend_own(where, chunk, q, kv):
    heads = GROUP // HD
    q_spec = pl.BlockSpec((ROWS, HD), lambda h, w: (0, heads * chunk + h))
    k_spec = pl.BlockSpec((ROWS, HD), lambda h, w: (0, h))
    v_spec = pl.BlockSpec((ROWS, HD), lambda h, w: (0, heads + h))
    return pl.pallas_call(
        own_kernel,
        grid_spec=pltpu.PrefetchScalarGridSpec(
            num_scalar_prefetch=1,
            grid=(heads,),
            in_specs=[q_spec] * 4 + [k_spec] * 4 + [v_spec] * 4,
            out_specs=[
                pl.BlockSpec((HD, SEQ_HALF), lambda h, w: (h, 0)),
                pl.BlockSpec((8, SEQ_HALF), lambda h, w: (0, 0)),
            ],
        ),
        out_shape=[
            jax.ShapeDtypeStruct((GROUP, SEQ_HALF), jnp.bfloat16),
            jax.ShapeDtypeStruct((8, SEQ_HALF), jnp.float32),
        ],
        compiler_params=pltpu.CompilerParams(vmem_limit_bytes=24 * 1024 * 1024),
        cost_estimate=attention_cost(heads),
        name="attend_own",
    )(where, *q, *kv, *kv)


def attend_far(where, q, kv):
    heads = GROUP // HD
    q_spec = pl.BlockSpec((SEQ_HALF, HD), lambda h, w: (0, h))
    k_spec = pl.BlockSpec((ROWS, HD), lambda h, w: (0, h))
    v_spec = pl.BlockSpec((ROWS, HD), lambda h, w: (0, heads + h))
    return pl.pallas_call(
        far_kernel,
        grid_spec=pltpu.PrefetchScalarGridSpec(
            num_scalar_prefetch=1,
            grid=(heads,),
            in_specs=[q_spec] + [k_spec] * 4 + [v_spec] * 4,
            out_specs=pl.BlockSpec((GROUP + 16, SEQ_HALF), lambda h, w: (0, 0)),
            scratch_shapes=[pltpu.VMEM((8, SEQ_HALF), jnp.float32)],
        ),
        out_shape=jax.ShapeDtypeStruct((GROUP + 16, SEQ_HALF), jnp.bfloat16),
        compiler_params=pltpu.CompilerParams(vmem_limit_bytes=24 * 1024 * 1024),
        cost_estimate=attention_cost(heads),
        name="attend_far",
    )(where, q, *kv, *kv)


def merge_kernel(where_ref, own_ref, far_ref, own_lse_ref, out_ref):
    terms = far_ref[pl.ds(GROUP, 16), :].astype(jnp.float32)
    far_lse = terms[0:4] + terms[4:8] + terms[8:12]
    far_lse = jnp.where(where_ref[1] == 1, far_lse, -1e30)
    own_lse = own_lse_ref[0:4, :]
    highest = jnp.maximum(own_lse, far_lse)
    own_part = jnp.exp2(own_lse - highest)
    far_part = jnp.exp2(far_lse - highest)
    total = own_part + far_part
    own_part = own_part / total
    far_part = far_part / total
    for head in range(GROUP // HD):
        rows = pl.ds(head * HD, HD)
        mixed = own_ref[rows, :].astype(jnp.float32) * own_part[head : head + 1]
        mixed = mixed + far_ref[rows, :].astype(jnp.float32) * far_part[head : head + 1]
        out_ref[:, rows] = mixed.T.astype(jnp.bfloat16)


def merge(where, own, far, own_lse):
    whole = pl.BlockSpec(memory_space=pltpu.VMEM)
    return pl.pallas_call(
        merge_kernel,
        in_specs=[pl.BlockSpec(memory_space=pltpu.SMEM), whole, whole, whole],
        out_specs=whole,
        out_shape=jax.ShapeDtypeStruct((SEQ_HALF, GROUP), jnp.bfloat16),
        compiler_params=pltpu.CompilerParams(vmem_limit_bytes=16 * 1024 * 1024),
        cost_estimate=pl.CostEstimate(flops=4 * 512 * 512, bytes_accessed=3 * 512 * 1024, transcendentals=0),
        name="merge_halves",
    )(where, own, far, own_lse)


def norm_kernel(where_ref, *refs):
    own_refs, peer_refs = refs[0:3], refs[3:6]
    res_ref, gain_ref, bias_ref, out_ref = refs[6:10]
    core, x = where_ref[2], where_ref[3]
    blocks = []
    for half, parts in ((core, own_refs), (1 - core, peer_refs)):
        for apart, part, column in ((0, 0, 0), (-1, 1, 0), (1, 1, 1), (2, 2, 0)):
            at = half * HALF + ((x + apart) & 3) * BLOCK
            at = pl.ds(pl.multiple_of(at, 128), BLOCK)
            added = parts[part][:, pl.ds(column * BLOCK, BLOCK)].astype(jnp.float32)
            blocks.append((at, deepnorm_alpha * res_ref[:, at].astype(jnp.float32) + added))
    mean = sum(jnp.sum(b, -1, keepdims=True) for _, b in blocks) / D
    blocks = [(at, b - mean) for at, b in blocks]
    var = sum(jnp.sum(b * b, -1, keepdims=True) for _, b in blocks) / D
    inv = lax.rsqrt(var + norm_eps)
    for at, b in blocks:
        out_ref[:, at] = (b * inv * gain_ref[:, at] + bias_ref[:, at]).astype(jnp.bfloat16)


def layer_norm(where, own, peer, residual, gain, bias):
    rows = 32
    parts = [pl.BlockSpec((rows, width), lambda i, w: (i, 0)) for width in (BLOCK, 2 * BLOCK, BLOCK)]
    full = pl.BlockSpec((rows, D), lambda i, w: (i, 0))
    vector = pl.BlockSpec((1, D), lambda i, w: (0, 0))
    return pl.pallas_call(
        norm_kernel,
        grid_spec=pltpu.PrefetchScalarGridSpec(
            num_scalar_prefetch=1,
            grid=(ROWS // rows,),
            in_specs=parts * 2 + [full, vector, vector],
            out_specs=full,
        ),
        out_shape=jax.ShapeDtypeStruct((ROWS, D), jnp.bfloat16),
        compiler_params=pltpu.CompilerParams(vmem_limit_bytes=24 * 1024 * 1024),
        cost_estimate=pl.CostEstimate(flops=10 * ROWS * D, bytes_accessed=6 * ROWS * D, transcendentals=0),
        name="layer_norm",
    )(where, *own, *peer, residual, gain.reshape(1, D), bias.reshape(1, D))


def after(value, *others):
    return lax.optimization_barrier((value, *others))[0]


def exchange_y(arrays, y, starts):
    parts = []
    for step in range(4):
        at = ((y + step) & 3) * GROUP
        part = jnp.concatenate(
            [lax.dynamic_slice_in_dim(a, s + at, GROUP, axis=1) for a, s in zip(arrays, starts)], axis=1
        )
        parts.append(part)
    return [parts[0]] + [lax.ppermute(parts[s], "y", ring(4, s)) for s in (1, 2, 3)]


def send(block, step):
    return lax.ppermute(block.astype(jnp.bfloat16), "y", ring(4, step))


def local(queries, keys, values, residual_in, out_weight, norm_gain, norm_bias):
    y = lax.axis_index("y")
    zh = lax.axis_index("zh")
    core = lax.axis_index("c")
    where = jnp.stack([y, zh, core, lax.axis_index("x")]).astype(jnp.int32)

    shard = lax.ppermute(out_weight.T, ("x", "zl", "c"), spread_pairs())
    weight = lax.all_gather(shard, ("zh", "zl"), axis=0, tiled=True)
    queries = after(queries, shard)

    q = exchange_y([queries, queries], y, [0, 2048])
    q_0 = jnp.concatenate([b[:, :GROUP] for b in q], axis=0)
    q_1 = jnp.concatenate([b[:, GROUP:] for b in q], axis=0)
    far_q0 = lax.ppermute(q_0, "zh", [(1, 0)])
    keys, values, *_ = lax.optimization_barrier((keys, values, *q))
    kv_0 = exchange_y([keys, values], y, [0, 0])
    far_q1 = lax.ppermute(after(q_1, far_q0), "zh", [(1, 0)])
    keys, values, *_ = lax.optimization_barrier((keys, values, *kv_0))
    kv_1 = exchange_y([keys, values], y, [2048, 2048])

    weight = after(weight, *kv_1).reshape(2, BLOCK, GROUP)
    left = lax.ppermute(weight, "x", ring(4, 1))
    right = lax.ppermute(weight, "x", ring(4, -1))
    far = jnp.stack([lax.ppermute(left[0], "x", ring(4, 1)), lax.ppermute(right[1], "x", ring(4, -1))])
    weights = [weight, jnp.concatenate([left, right], axis=1), far]

    outs = []
    peers = []
    for chunk, far_q, kv in ((0, far_q0, kv_0), (1, far_q1, kv_1)):
        far_out = attend_far(where, far_q, kv)
        far_out = lax.ppermute(far_out, "zh", [(0, 1)])
        own_out, own_lse = attend_own(where, chunk, q, kv)
        out = merge(where, own_out, far_out, own_lse)
        outs.append(out)
        peers.append(lax.ppermute(out, "c", ring(2, 1)))
    own, other = (
        [jnp.concatenate([part[s * ROWS : (s + 1) * ROWS] for part in parts], axis=1) for s in range(4)]
        for parts in (outs, peers)
    )

    sums = []
    peer_sums = []
    for weight in weights:

        def project(heads):
            return lax.dot_general(
                heads.reshape(ROWS, 2, GROUP), weight, (((1, 2), (0, 2)), ((), ())),
                preferred_element_type=jnp.float32,
            )

        up_1 = send(project(own[2]), 1)
        down_1 = send(project(other[2]), -1)
        up_2 = send(project(other[3]), 1)
        down_2 = send(project(own[1]), -1)
        up_3 = send(project(own[3]) + up_1.astype(jnp.float32), 1)
        down_3 = send(project(other[1]) + down_1.astype(jnp.float32), -1)
        total_other = project(other[0]) + up_2.astype(jnp.float32) + down_3.astype(jnp.float32)
        peer_sums.append(lax.ppermute(total_other.astype(jnp.bfloat16), "c", ring(2, 1)))
        total_own = project(own[0]) + down_2.astype(jnp.float32) + up_3.astype(jnp.float32)
        sums.append(total_own.astype(jnp.bfloat16))
        *heads, _, _ = lax.optimization_barrier((*own, *other, up_1, down_1))
        own, other = heads[:4], heads[4:]
    return layer_norm(where, sums, peer_sums, residual_in, norm_gain, norm_bias)


def solution(mesh):
    fine = Mesh(mesh.devices.reshape(4, 4, 2, 2, 4), AXES)
    tokens = P(AXES, None)
    in_specs = (tokens, tokens, tokens, tokens, P(("zh", "y"), ("x", "zl", "c")), P(), P())
    return jax.shard_map(local, mesh=fine, in_specs=in_specs, out_specs=tokens, check_vma=False)
```

```python
import functools
import math

import jax
import jax.numpy as jnp
from jax import lax
from jax.experimental import pallas as pl
from jax.experimental.pallas import tpu as pltpu
from jax.sharding import Mesh, PartitionSpec as P

HD = 128
GROUP = 512
ROWS = 128
SEQ_HALF = 512
D = 7168
HALF = D // 2
BLOCK = HALF // 4

deepnorm_alpha = 96.0**0.25
norm_eps = 1e-05
score_scale = math.log2(math.e) / math.sqrt(HD)

AXES = ("x", "zl", "c", "zh", "y")


def ring(n, step):
    return [(i, (i + step) % n) for i in range(n)]


def z_ring(step):
    pairs = []
    for z in range(8):
        to = (z + step) % 8
        pairs.append(((z % 4) * 2 + z // 4, (to % 4) * 2 + to // 4))
    return pairs


def spread_pairs():
    return [(s, (s % 4) * 2 + s // 4) for s in range(8)]


def softmax_part(q, k, v, keep):
    scores = lax.dot_general(k, q, (((1,), (1,)), ((), ())), preferred_element_type=jnp.float32)
    if keep is not None:
        scores = jnp.where(keep, scores, -1e30)
    highest = jnp.max(scores, axis=0, keepdims=True)
    expo = jnp.exp2((scores - highest) * score_scale)
    total = jnp.sum(expo, axis=0, keepdims=True)
    out = lax.dot_general(
        v, expo.astype(jnp.bfloat16), (((0,), (0,)), ((), ())), preferred_element_type=jnp.float32
    )
    return (out / total).astype(jnp.bfloat16), highest * score_scale + jnp.log2(total)


def own_kernel(where_ref, *refs):
    q_refs, k_refs, v_refs, o_ref, lse_ref = refs[0:4], refs[4:8], refs[8:12], refs[12], refs[13]
    head = pl.program_id(0)
    y = where_ref[0]
    q, k, v = (jnp.concatenate([r[...] for r in part], axis=0) for part in (q_refs, k_refs, v_refs))

    def position(axis):
        at = lax.broadcasted_iota(jnp.int32, (SEQ_HALF, SEQ_HALF), axis)
        return ((y - at // ROWS) & 3) * ROWS + (at & (ROWS - 1))

    out, lse = softmax_part(q, k, v, position(0) <= position(1))
    o_ref[...] = out
    lse_ref[pl.ds(head, 1), :] = lse


def far_kernel(where_ref, q_ref, *refs):
    k_refs, v_refs, o_ref, lse_ref = refs[0:4], refs[4:8], refs[8], refs[9]
    head = pl.program_id(0)

    @pl.when(where_ref[1] == 0)
    def _():
        k, v = (jnp.concatenate([r[...] for r in part], axis=0) for part in (k_refs, v_refs))
        out, lse = softmax_part(q_ref[...], k, v, None)
        o_ref[pl.ds(pl.multiple_of(head * HD, HD), HD), :] = out
        lse_ref[pl.ds(head, 1), :] = lse

        @pl.when(head == GROUP // HD - 1)
        def _():
            rest = lse_ref[0:4, :]
            terms = []
            for _ in range(3):
                term = rest.astype(jnp.bfloat16).astype(jnp.float32)
                terms.append(term)
                rest = rest - term
            terms.append(jnp.zeros_like(rest))
            o_ref[pl.ds(GROUP, 16), :] = jnp.concatenate(terms, axis=0).astype(jnp.bfloat16)


def attention_cost(heads):
    return pl.CostEstimate(
        flops=heads * 4 * SEQ_HALF * SEQ_HALF * HD, bytes_accessed=2 * 1024 * 1024,
        transcendentals=heads * SEQ_HALF * SEQ_HALF)


def attend_own(where, chunk, q, kv):
    heads = GROUP // HD
    q_spec = pl.BlockSpec((ROWS, HD), lambda h, w: (0, heads * chunk + h))
    k_spec = pl.BlockSpec((ROWS, HD), lambda h, w: (0, h))
    v_spec = pl.BlockSpec((ROWS, HD), lambda h, w: (0, heads + h))
    return pl.pallas_call(
        own_kernel,
        grid_spec=pltpu.PrefetchScalarGridSpec(
            num_scalar_prefetch=1,
            grid=(heads,),
            in_specs=[q_spec] * 4 + [k_spec] * 4 + [v_spec] * 4,
            out_specs=[
                pl.BlockSpec((HD, SEQ_HALF), lambda h, w: (h, 0)),
                pl.BlockSpec((8, SEQ_HALF), lambda h, w: (0, 0)),
            ],
        ),
        out_shape=[
            jax.ShapeDtypeStruct((GROUP, SEQ_HALF), jnp.bfloat16),
            jax.ShapeDtypeStruct((8, SEQ_HALF), jnp.float32),
        ],
        compiler_params=pltpu.CompilerParams(vmem_limit_bytes=24 * 1024 * 1024),
        cost_estimate=attention_cost(heads),
        name="attend_own",
    )(where, *q, *kv, *kv)


def attend_far(where, q, kv):
    heads = GROUP // HD
    q_spec = pl.BlockSpec((SEQ_HALF, HD), lambda h, w: (0, h))
    k_spec = pl.BlockSpec((ROWS, HD), lambda h, w: (0, h))
    v_spec = pl.BlockSpec((ROWS, HD), lambda h, w: (0, heads + h))
    return pl.pallas_call(
        far_kernel,
        grid_spec=pltpu.PrefetchScalarGridSpec(
            num_scalar_prefetch=1,
            grid=(heads,),
            in_specs=[q_spec] + [k_spec] * 4 + [v_spec] * 4,
            out_specs=pl.BlockSpec((GROUP + 16, SEQ_HALF), lambda h, w: (0, 0)),
            scratch_shapes=[pltpu.VMEM((8, SEQ_HALF), jnp.float32)],
        ),
        out_shape=jax.ShapeDtypeStruct((GROUP + 16, SEQ_HALF), jnp.bfloat16),
        compiler_params=pltpu.CompilerParams(vmem_limit_bytes=24 * 1024 * 1024),
        cost_estimate=attention_cost(heads),
        name="attend_far",
    )(where, q, *kv, *kv)


def merge_kernel(where_ref, own_ref, far_ref, own_lse_ref, out_ref):
    terms = far_ref[pl.ds(GROUP, 16), :].astype(jnp.float32)
    far_lse = terms[0:4] + terms[4:8] + terms[8:12]
    far_lse = jnp.where(where_ref[1] == 1, far_lse, -1e30)
    own_lse = own_lse_ref[0:4, :]
    highest = jnp.maximum(own_lse, far_lse)
    own_part = jnp.exp2(own_lse - highest)
    far_part = jnp.exp2(far_lse - highest)
    total = own_part + far_part
    own_part = own_part / total
    far_part = far_part / total
    for head in range(GROUP // HD):
        rows = pl.ds(head * HD, HD)
        mixed = own_ref[rows, :].astype(jnp.float32) * own_part[head : head + 1]
        mixed = mixed + far_ref[rows, :].astype(jnp.float32) * far_part[head : head + 1]
        out_ref[:, rows] = mixed.T.astype(jnp.bfloat16)


def merge(where, own, far, own_lse):
    whole = pl.BlockSpec(memory_space=pltpu.VMEM)
    return pl.pallas_call(
        merge_kernel,
        in_specs=[pl.BlockSpec(memory_space=pltpu.SMEM), whole, whole, whole],
        out_specs=whole,
        out_shape=jax.ShapeDtypeStruct((SEQ_HALF, GROUP), jnp.bfloat16),
        compiler_params=pltpu.CompilerParams(vmem_limit_bytes=16 * 1024 * 1024),
        cost_estimate=pl.CostEstimate(flops=4 * 512 * 512, bytes_accessed=3 * 512 * 1024, transcendentals=0),
        name="merge_halves",
    )(where, own, far, own_lse)


def norm_kernel(where_ref, *refs):
    own_refs, peer_refs = refs[0:2], refs[2:4]
    res_ref, gain_ref, bias_ref, out_ref = refs[4:8]
    core, x = where_ref[2], where_ref[3]
    blocks = []
    for half, parts in ((core, own_refs), (1 - core, peer_refs)):
        for apart, part, column in ((0, 0, 0), (-1, 0, 1), (1, 1, 0), (2, 1, 1)):
            at = ((x + apart) & 3) * (2 * BLOCK) + half * BLOCK
            at = pl.ds(pl.multiple_of(at, 128), BLOCK)
            added = parts[part][:, pl.ds(column * BLOCK, BLOCK)].astype(jnp.float32)
            blocks.append((at, deepnorm_alpha * res_ref[:, at].astype(jnp.float32) + added))
    mean = sum(jnp.sum(b, -1, keepdims=True) for _, b in blocks) / D
    blocks = [(at, b - mean) for at, b in blocks]
    var = sum(jnp.sum(b * b, -1, keepdims=True) for _, b in blocks) / D
    inv = lax.rsqrt(var + norm_eps)
    for at, b in blocks:
        out_ref[:, at] = (b * inv * gain_ref[:, at] + bias_ref[:, at]).astype(jnp.bfloat16)


def layer_norm(where, own, peer, residual, gain, bias):
    rows = 32
    part = pl.BlockSpec((rows, 2 * BLOCK), lambda i, w: (i, 0))
    full = pl.BlockSpec((rows, D), lambda i, w: (i, 0))
    vector = pl.BlockSpec((1, D), lambda i, w: (0, 0))
    return pl.pallas_call(
        norm_kernel,
        grid_spec=pltpu.PrefetchScalarGridSpec(
            num_scalar_prefetch=1,
            grid=(ROWS // rows,),
            in_specs=[part] * 4 + [full, vector, vector],
            out_specs=full,
        ),
        out_shape=jax.ShapeDtypeStruct((ROWS, D), jnp.bfloat16),
        compiler_params=pltpu.CompilerParams(vmem_limit_bytes=24 * 1024 * 1024),
        cost_estimate=pl.CostEstimate(flops=10 * ROWS * D, bytes_accessed=6 * ROWS * D, transcendentals=0),
        name="layer_norm",
    )(where, *own, *peer, residual, gain.reshape(1, D), bias.reshape(1, D))


def after(value, *others):
    return lax.optimization_barrier((value, *others))[0]


def columns_for(arrays, y, starts):
    return [
        jnp.concatenate(
            [lax.dynamic_slice_in_dim(a, s + ((y + step) & 3) * GROUP, GROUP, axis=1) for a, s in zip(arrays, starts)],
            axis=1,
        )
        for step in range(4)
    ]


def forward(part, step):
    return lax.ppermute(part, "y", ring(4, step))


def put(column, part, at):
    return lax.dynamic_update_slice(column, part[None], (at & 7, 0, 0))


def send(block, step):
    return lax.ppermute(block.astype(jnp.bfloat16), "y", ring(4, step))


def local(queries, keys, values, residual_in, out_weight, norm_gain, norm_bias):
    y = lax.axis_index("y")
    zh = lax.axis_index("zh")
    core = lax.axis_index("c")
    where = jnp.stack([y, zh, core, lax.axis_index("x")]).astype(jnp.int32)

    z = zh * 4 + lax.axis_index("zl")
    up_z = functools.partial(lax.ppermute, axis_name=("zl", "zh"), perm=z_ring(1))
    down_z = functools.partial(lax.ppermute, axis_name=("zl", "zh"), perm=z_ring(-1))

    q = columns_for([queries, queries], y, [0, 2048])
    q = [q[0]] + [forward(q[s], s) for s in (1, 2, 3)]
    shard = lax.ppermute(out_weight.T, ("zl", "c"), spread_pairs())
    up = [shard, up_z(shard)]
    down = [shard, down_z(shard)]

    q_0 = jnp.concatenate([b[:, :GROUP] for b in q], axis=0)
    q_1 = jnp.concatenate([b[:, GROUP:] for b in q], axis=0)
    far_q0 = lax.ppermute(q_0, "zh", [(1, 0)])
    keys, values, up[1], down[1], *_ = lax.optimization_barrier((keys, values, up[1], down[1], *q))
    kv_0 = columns_for([keys, values], y, [0, 0])
    kv_0[1], kv_0[3] = forward(kv_0[1], 1), forward(kv_0[3], 3)
    up.append(up_z(up[1]))
    down.append(down_z(down[1]))

    keys, values, up[2], down[2], kv_0[1], kv_0[3], kv_0[2] = lax.optimization_barrier(
        (keys, values, up[2], down[2], kv_0[1], kv_0[3], kv_0[2])
    )
    kv_1 = columns_for([keys, values], y, [2048, 2048])
    kv_0[2] = forward(kv_0[2], 2)
    kv_1[1] = forward(kv_1[1], 1)
    up.append(up_z(up[2]))
    down.append(down_z(down[2]))

    kv_1[3], kv_1[2], up[3], *_ = lax.optimization_barrier((kv_1[3], kv_1[2], up[3], kv_0[2], kv_1[1], down[3]))
    far_q1 = lax.ppermute(after(q_1, far_q0), "zh", [(1, 0)])
    up.append(up_z(up[3]))
    kv_1[3] = forward(kv_1[3], 3)
    kv_1[2] = forward(kv_1[2], 2)

    weight = jnp.zeros((8, 224, GROUP), jnp.bfloat16)
    for step in range(5):
        weight = put(weight, up[step], z - step)
        if 0 < step < 4:
            weight = put(weight, down[step], z + step)
    weight = weight.reshape(2, BLOCK, GROUP)
    left = lax.ppermute(weight, "x", ring(4, 1))
    right = lax.ppermute(weight, "x", ring(4, -1))
    far = jnp.stack([lax.ppermute(left[0], "x", ring(4, 1)), lax.ppermute(right[1], "x", ring(4, -1))])
    weights = [jnp.concatenate([weight, left], axis=1), jnp.concatenate([right, far], axis=1)]

    outs = []
    peers = []
    for chunk, far_q, kv in ((0, far_q0, kv_0), (1, far_q1, kv_1)):
        far_out = attend_far(where, far_q, kv)
        far_out = lax.ppermute(far_out, "zh", [(0, 1)])
        own_out, own_lse = attend_own(where, chunk, q, kv)
        out = merge(where, own_out, far_out, own_lse)
        outs.append(out)
        peers.append(lax.ppermute(out, "c", ring(2, 1)))
    own, other = (
        [jnp.concatenate([part[s * ROWS : (s + 1) * ROWS] for part in parts], axis=1) for s in range(4)]
        for parts in (outs, peers)
    )

    sums = []
    peer_sums = []
    for weight in weights:

        def project(heads):
            return lax.dot_general(
                heads.reshape(ROWS, 2, GROUP), weight, (((1, 2), (0, 2)), ((), ())),
                preferred_element_type=jnp.float32,
            )

        up_1 = send(project(own[2]), 1)
        down_1 = send(project(other[2]), -1)
        up_2 = send(project(other[3]), 1)
        down_2 = send(project(own[1]), -1)
        up_3 = send(project(own[3]) + up_1.astype(jnp.float32), 1)
        down_3 = send(project(other[1]) + down_1.astype(jnp.float32), -1)
        total_other = project(other[0]) + up_2.astype(jnp.float32) + down_3.astype(jnp.float32)
        peer_sums.append(lax.ppermute(total_other.astype(jnp.bfloat16), "c", ring(2, 1)))
        total_own = project(own[0]) + down_2.astype(jnp.float32) + up_3.astype(jnp.float32)
        sums.append(total_own.astype(jnp.bfloat16))
        own[2], other[2], _, _ = lax.optimization_barrier((own[2], other[2], up_2, down_2))
        own[1], other[3], _, _ = lax.optimization_barrier((own[1], other[3], up_3, down_3))
    return layer_norm(where, sums, peer_sums, residual_in, norm_gain, norm_bias)


def solution(mesh):
    fine = Mesh(mesh.devices.reshape(4, 4, 2, 2, 4), AXES)
    tokens = P(AXES, None)
    in_specs = (tokens, tokens, tokens, tokens, P(("zh", "y"), ("x", "zl", "c")), P(), P())
    return jax.shard_map(local, mesh=fine, in_specs=in_specs, out_specs=tokens, check_vma=False)
```

```python
import functools
import math

import jax
import jax.numpy as jnp
from jax import lax
from jax.experimental import pallas as pl
from jax.experimental.pallas import tpu as pltpu
from jax.sharding import Mesh, PartitionSpec as P

HD = 128
GROUP = 512
ROWS = 128
SEQ_HALF = 512
D = 7168
HALF = D // 2
BLOCK = HALF // 4

deepnorm_alpha = 96.0**0.25
norm_eps = 1e-05
score_scale = math.log2(math.e) / math.sqrt(HD)

AXES = ("x", "zl", "c", "zh", "y")


def ring(n, step):
    return [(i, (i + step) % n) for i in range(n)]


def z_ring(step):
    pairs = []
    for z in range(8):
        to = (z + step) % 8
        pairs.append(((z % 4) * 2 + z // 4, (to % 4) * 2 + to // 4))
    return pairs


def softmax_part(q, k, v, keep):
    scores = lax.dot_general(k, q, (((1,), (1,)), ((), ())), preferred_element_type=jnp.float32)
    if keep is not None:
        scores = jnp.where(keep, scores, -1e30)
    highest = jnp.max(scores, axis=0, keepdims=True)
    expo = jnp.exp2((scores - highest) * score_scale)
    total = jnp.sum(expo, axis=0, keepdims=True)
    out = lax.dot_general(
        v, expo.astype(jnp.bfloat16), (((0,), (0,)), ((), ())), preferred_element_type=jnp.float32
    )
    return (out / total).astype(jnp.bfloat16), highest * score_scale + jnp.log2(total)


def own_kernel(where_ref, *refs):
    q_refs, k_refs, v_refs, o_ref, lse_ref = refs[0:4], refs[4:8], refs[8:12], refs[12], refs[13]
    head = pl.program_id(0)
    y = where_ref[0]
    q, k, v = (jnp.concatenate([r[...] for r in part], axis=0) for part in (q_refs, k_refs, v_refs))

    def position(axis):
        at = lax.broadcasted_iota(jnp.int32, (SEQ_HALF, SEQ_HALF), axis)
        return ((y - at // ROWS) & 3) * ROWS + (at & (ROWS - 1))

    out, lse = softmax_part(q, k, v, position(0) <= position(1))
    o_ref[...] = out
    lse_ref[pl.ds(head, 1), :] = lse


def far_kernel(at_half, where_ref, q_ref, *refs):
    *kv_refs, o_ref, lse_ref = refs
    count = len(kv_refs) // 2
    k_refs, v_refs = kv_refs[:count], kv_refs[count:]
    head = pl.program_id(0)

    @pl.when(where_ref[1] == at_half)
    def _():
        k, v = (jnp.concatenate([r[...] for r in part], axis=0) for part in (k_refs, v_refs))
        out, lse = softmax_part(q_ref[...], k, v, None)
        o_ref[pl.ds(pl.multiple_of(head * HD, HD), HD), :] = out
        lse_ref[pl.ds(head, 1), :] = lse

        @pl.when(head == GROUP // HD - 1)
        def _():
            rest = lse_ref[0:4, :]
            terms = []
            for _ in range(3):
                term = rest.astype(jnp.bfloat16).astype(jnp.float32)
                terms.append(term)
                rest = rest - term
            terms.append(jnp.zeros_like(rest))
            o_ref[pl.ds(GROUP, 16), :] = jnp.concatenate(terms, axis=0).astype(jnp.bfloat16)


def attention_cost(heads):
    return pl.CostEstimate(
        flops=heads * 4 * SEQ_HALF * SEQ_HALF * HD, bytes_accessed=2 * 1024 * 1024,
        transcendentals=heads * SEQ_HALF * SEQ_HALF)


def attend_own(where, chunk, q, kv):
    heads = GROUP // HD
    q_spec = pl.BlockSpec((ROWS, HD), lambda h, w: (0, heads * chunk + h))
    k_spec = pl.BlockSpec((ROWS, HD), lambda h, w: (0, h))
    v_spec = pl.BlockSpec((ROWS, HD), lambda h, w: (0, heads + h))
    return pl.pallas_call(
        own_kernel,
        grid_spec=pltpu.PrefetchScalarGridSpec(
            num_scalar_prefetch=1,
            grid=(heads,),
            in_specs=[q_spec] * 4 + [k_spec] * 4 + [v_spec] * 4,
            out_specs=[
                pl.BlockSpec((HD, SEQ_HALF), lambda h, w: (h, 0)),
                pl.BlockSpec((8, SEQ_HALF), lambda h, w: (0, 0)),
            ],
        ),
        out_shape=[
            jax.ShapeDtypeStruct((GROUP, SEQ_HALF), jnp.bfloat16),
            jax.ShapeDtypeStruct((8, SEQ_HALF), jnp.float32),
        ],
        compiler_params=pltpu.CompilerParams(vmem_limit_bytes=24 * 1024 * 1024),
        cost_estimate=attention_cost(heads),
        name="attend_own",
    )(where, *q, *kv, *kv)


def attend_far(where, at_half, q, kv):
    heads = GROUP // HD
    count = len(kv)
    q_spec = pl.BlockSpec((SEQ_HALF, HD), lambda h, w: (0, h))
    k_spec = pl.BlockSpec((SEQ_HALF // count, HD), lambda h, w: (0, h))
    v_spec = pl.BlockSpec((SEQ_HALF // count, HD), lambda h, w: (0, heads + h))
    return pl.pallas_call(
        functools.partial(far_kernel, at_half),
        grid_spec=pltpu.PrefetchScalarGridSpec(
            num_scalar_prefetch=1,
            grid=(heads,),
            in_specs=[q_spec] + [k_spec] * count + [v_spec] * count,
            out_specs=pl.BlockSpec((GROUP + 16, SEQ_HALF), lambda h, w: (0, 0)),
            scratch_shapes=[pltpu.VMEM((8, SEQ_HALF), jnp.float32)],
        ),
        out_shape=jax.ShapeDtypeStruct((GROUP + 16, SEQ_HALF), jnp.bfloat16),
        compiler_params=pltpu.CompilerParams(vmem_limit_bytes=24 * 1024 * 1024),
        cost_estimate=attention_cost(heads),
        name="attend_far",
    )(where, q, *kv, *kv)


def merge_kernel(where_ref, own_ref, far_ref, own_lse_ref, out_ref):
    terms = far_ref[pl.ds(GROUP, 16), :].astype(jnp.float32)
    far_lse = terms[0:4] + terms[4:8] + terms[8:12]
    far_lse = jnp.where(where_ref[1] == 1, far_lse, -1e30)
    own_lse = own_lse_ref[0:4, :]
    highest = jnp.maximum(own_lse, far_lse)
    own_part = jnp.exp2(own_lse - highest)
    far_part = jnp.exp2(far_lse - highest)
    total = own_part + far_part
    own_part = own_part / total
    far_part = far_part / total
    for head in range(GROUP // HD):
        rows = pl.ds(head * HD, HD)
        mixed = own_ref[rows, :].astype(jnp.float32) * own_part[head : head + 1]
        far = jnp.where(where_ref[1] == 1, far_ref[rows, :].astype(jnp.float32), 0.0)
        mixed = mixed + far * far_part[head : head + 1]
        out_ref[:, rows] = mixed.T.astype(jnp.bfloat16)


def merge(where, own, far, own_lse):
    whole = pl.BlockSpec(memory_space=pltpu.VMEM)
    return pl.pallas_call(
        merge_kernel,
        in_specs=[pl.BlockSpec(memory_space=pltpu.SMEM), whole, whole, whole],
        out_specs=whole,
        out_shape=jax.ShapeDtypeStruct((SEQ_HALF, GROUP), jnp.bfloat16),
        compiler_params=pltpu.CompilerParams(vmem_limit_bytes=16 * 1024 * 1024),
        cost_estimate=pl.CostEstimate(flops=4 * 512 * 512, bytes_accessed=3 * 512 * 1024, transcendentals=0),
        name="merge_halves",
    )(where, own, far, own_lse)


def norm_kernel(where_ref, *refs):
    own_refs, peer_refs = refs[0:2], refs[2:4]
    res_ref, gain_ref, bias_ref, out_ref = refs[4:8]
    core, x = where_ref[2], where_ref[3]
    blocks = []
    for half, parts in ((core, own_refs), (1 - core, peer_refs)):
        for apart, part, column in ((0, 0, 0), (-1, 0, 1), (1, 1, 0), (2, 1, 1)):
            at = ((x + apart) & 3) * (2 * BLOCK) + half * BLOCK
            at = pl.ds(pl.multiple_of(at, 128), BLOCK)
            added = parts[part][:, pl.ds(column * BLOCK, BLOCK)].astype(jnp.float32)
            blocks.append((at, deepnorm_alpha * res_ref[:, at].astype(jnp.float32) + added))
    mean = sum(jnp.sum(b, -1, keepdims=True) for _, b in blocks) / D
    blocks = [(at, b - mean) for at, b in blocks]
    var = sum(jnp.sum(b * b, -1, keepdims=True) for _, b in blocks) / D
    inv = lax.rsqrt(var + norm_eps)
    for at, b in blocks:
        out_ref[:, at] = (b * inv * gain_ref[:, at] + bias_ref[:, at]).astype(jnp.bfloat16)


def layer_norm(where, own, peer, residual, gain, bias):
    rows = 32
    part = pl.BlockSpec((rows, 2 * BLOCK), lambda i, w: (i, 0))
    full = pl.BlockSpec((rows, D), lambda i, w: (i, 0))
    vector = pl.BlockSpec((1, D), lambda i, w: (0, 0))
    return pl.pallas_call(
        norm_kernel,
        grid_spec=pltpu.PrefetchScalarGridSpec(
            num_scalar_prefetch=1,
            grid=(ROWS // rows,),
            in_specs=[part] * 4 + [full, vector, vector],
            out_specs=full,
        ),
        out_shape=jax.ShapeDtypeStruct((ROWS, D), jnp.bfloat16),
        compiler_params=pltpu.CompilerParams(vmem_limit_bytes=24 * 1024 * 1024),
        cost_estimate=pl.CostEstimate(flops=10 * ROWS * D, bytes_accessed=6 * ROWS * D, transcendentals=0),
        name="layer_norm",
    )(where, *own, *peer, residual, gain.reshape(1, D), bias.reshape(1, D))


def after(value, *others):
    return lax.optimization_barrier((value, *others))[0]


def columns_for(arrays, y, starts):
    return [
        jnp.concatenate(
            [lax.dynamic_slice_in_dim(a, s + ((y + step) & 3) * GROUP, GROUP, axis=1) for a, s in zip(arrays, starts)],
            axis=1,
        )
        for step in range(4)
    ]


def forward(part, step):
    return lax.ppermute(part, "y", ring(4, step))


def put(column, part, at):
    return lax.dynamic_update_slice(column, part[None], (at & 7, 0, 0))


def send(block, step):
    return lax.ppermute(block.astype(jnp.bfloat16), "y", ring(4, step))


def local(queries, keys, values, residual_in, out_weight, norm_gain, norm_bias):
    y = lax.axis_index("y")
    zh = lax.axis_index("zh")
    core = lax.axis_index("c")
    where = jnp.stack([y, zh, core, lax.axis_index("x")]).astype(jnp.int32)

    z = zh * 4 + lax.axis_index("zl")
    up_z = functools.partial(lax.ppermute, axis_name=("zl", "zh"), perm=z_ring(1))
    down_z = functools.partial(lax.ppermute, axis_name=("zl", "zh"), perm=z_ring(-1))

    shard = out_weight.T
    up = [shard, up_z(shard)]
    down = [shard, down_z(shard)]
    q = columns_for([queries, queries], y, [0, 2048])
    q = [q[0]] + [forward(q[s], s) for s in (1, 2, 3)]
    up.append(up_z(up[1]))
    down.append(down_z(down[1]))

    up[2], down[2], keys, values, *_ = lax.optimization_barrier((up[2], down[2], keys, values, *q))
    up.append(up_z(up[2]))
    down.append(down_z(down[2]))
    kv_1 = columns_for([keys, values], y, [2048, 2048])
    kv_1 = [kv_1[0]] + [forward(kv_1[s], s) for s in (1, 2, 3)]
    up.append(up_z(up[3]))

    q_0 = jnp.concatenate([b[:, :GROUP] for b in q], axis=0)
    q_1 = jnp.concatenate([b[:, GROUP:] for b in q], axis=0)
    q_0, far_kv1, keys, values, _, _ = lax.optimization_barrier(
        (q_0, jnp.concatenate(kv_1, axis=0), keys, values, up[4], down[3])
    )
    far_q0 = lax.ppermute(q_0, "zh", [(1, 0)])
    far_kv1 = lax.ppermute(far_kv1, "zh", [(0, 1)])
    kv_0 = columns_for([keys, values], y, [0, 0])
    kv_0 = [kv_0[0]] + [forward(kv_0[s], s) for s in (1, 2, 3)]

    weight = jnp.zeros((8, 224, GROUP), jnp.bfloat16)
    for step in range(5):
        weight = put(weight, up[step], z - step)
        if 0 < step < 4:
            weight = put(weight, down[step], z + step)
    weight = weight.reshape(2, 2, 2, 224, GROUP)
    mine = lax.dynamic_index_in_dim(weight, core, 1, keepdims=False)
    theirs = lax.ppermute(lax.dynamic_index_in_dim(weight, 1 - core, 1, keepdims=False), "c", ring(2, 1))
    first = jnp.where(core == 0, mine, theirs)
    second = jnp.where(core == 0, theirs, mine)
    weight = jnp.stack([first, second], axis=2).reshape(2, BLOCK, GROUP)
    weight = after(weight, kv_0[1], kv_0[2], kv_0[3])
    left = lax.ppermute(weight, "x", ring(4, 1))
    right = lax.ppermute(weight, "x", ring(4, -1))
    far = jnp.stack([lax.ppermute(left[0], "x", ring(4, 1)), lax.ppermute(right[1], "x", ring(4, -1))])
    weights = [jnp.concatenate([weight, left], axis=1), jnp.concatenate([right, far], axis=1)]

    own_1, lse_1 = attend_own(where, 1, q, kv_1)
    far_0 = lax.ppermute(attend_far(where, 0, far_q0, kv_0), "zh", [(0, 1)])
    far_1 = attend_far(where, 1, q_1, [far_kv1])
    own_0, lse_0 = attend_own(where, 0, q, kv_0)
    out_1 = merge(where, own_1, far_1, lse_1)
    out_0 = merge(where, own_0, far_0, lse_0)
    outs = [out_0, out_1]
    peers = [lax.ppermute(out, "c", ring(2, 1)) for out in outs]
    own, other = (
        [jnp.concatenate([part[s * ROWS : (s + 1) * ROWS] for part in parts], axis=1) for s in range(4)]
        for parts in (outs, peers)
    )

    sums = []
    peer_sums = []
    for weight in weights:

        def project(heads):
            return lax.dot_general(
                heads.reshape(ROWS, 2, GROUP), weight, (((1, 2), (0, 2)), ((), ())),
                preferred_element_type=jnp.float32,
            )

        up_1 = send(project(own[2]), 1)
        down_1 = send(project(other[2]), -1)
        up_2 = send(project(other[3]), 1)
        down_2 = send(project(own[1]), -1)
        up_3 = send(project(own[3]) + up_1.astype(jnp.float32), 1)
        down_3 = send(project(other[1]) + down_1.astype(jnp.float32), -1)
        total_other = project(other[0]) + up_2.astype(jnp.float32) + down_3.astype(jnp.float32)
        peer_sums.append(lax.ppermute(total_other.astype(jnp.bfloat16), "c", ring(2, 1)))
        total_own = project(own[0]) + down_2.astype(jnp.float32) + up_3.astype(jnp.float32)
        sums.append(total_own.astype(jnp.bfloat16))
        own[2], other[2], _, _ = lax.optimization_barrier((own[2], other[2], up_2, down_2))
        own[1], other[3], _, _ = lax.optimization_barrier((own[1], other[3], up_3, down_3))
    return layer_norm(where, sums, peer_sums, residual_in, norm_gain, norm_bias)


def solution(mesh):
    fine = Mesh(mesh.devices.reshape(4, 4, 2, 2, 4), AXES)
    tokens = P(AXES, None)
    in_specs = (tokens, tokens, tokens, tokens, P(("zh", "y"), ("x", "zl", "c")), P(), P())
    return jax.shard_map(local, mesh=fine, in_specs=in_specs, out_specs=tokens, check_vma=False)
```

```python
import functools
import math

import jax
import jax.numpy as jnp
from jax import lax
from jax.experimental import pallas as pl
from jax.experimental.pallas import tpu as pltpu
from jax.sharding import Mesh, PartitionSpec as P

HD = 128
GROUP = 512
ROWS = 128
SEQ_HALF = 512
PAIR = 2 * HD
D = 7168
HALF = D // 2
BLOCK = HALF // 4

deepnorm_alpha = 96.0**0.25
norm_eps = 1e-05
score_scale = math.log2(math.e) / math.sqrt(HD)

AXES = ("x", "zl", "c", "zh", "y")


def ring(n, step):
    return [(i, (i + step) % n) for i in range(n)]


def z_ring(step):
    pairs = []
    for z in range(8):
        to = (z + step) % 8
        pairs.append(((z % 4) * 2 + z // 4, (to % 4) * 2 + to // 4))
    return pairs


def softmax_part(q, k, v, keep):
    scores = lax.dot_general(k, q, (((1,), (1,)), ((), ())), preferred_element_type=jnp.float32)
    if keep is not None:
        scores = jnp.where(keep, scores, -1e30)
    highest = jnp.max(scores, axis=0, keepdims=True)
    expo = jnp.exp2((scores - highest) * score_scale)
    total = jnp.sum(expo, axis=0, keepdims=True)
    out = lax.dot_general(
        v, expo.astype(jnp.bfloat16), (((0,), (0,)), ((), ())), preferred_element_type=jnp.float32
    )
    return (out / total).astype(jnp.bfloat16), highest * score_scale + jnp.log2(total)


def own_kernel(where_ref, *refs):
    q_refs, k_refs, v_refs, o_ref, lse_ref = refs[0:4], refs[4:8], refs[8:12], refs[12], refs[13]
    head = pl.program_id(0)
    y = where_ref[0]
    q, k, v = (jnp.concatenate([r[...] for r in part], axis=0) for part in (q_refs, k_refs, v_refs))

    def position(axis):
        at = lax.broadcasted_iota(jnp.int32, (SEQ_HALF, SEQ_HALF), axis)
        return ((y - at // ROWS) & 3) * ROWS + (at & (ROWS - 1))

    out, lse = softmax_part(q, k, v, position(0) <= position(1))
    o_ref[...] = out
    lse_ref[pl.ds(head, 1), :] = lse


def far_kernel(at_half, heads, where_ref, q_ref, *refs):
    *kv_refs, o_ref, lse_ref = refs
    count = len(kv_refs) // 2
    k_refs, v_refs = kv_refs[:count], kv_refs[count:]
    head = pl.program_id(0)

    @pl.when(where_ref[1] == at_half)
    def _():
        k, v = (jnp.concatenate([r[...] for r in part], axis=0) for part in (k_refs, v_refs))
        out, lse = softmax_part(q_ref[...], k, v, None)
        o_ref[pl.ds(pl.multiple_of(head * HD, HD), HD), :] = out
        lse_ref[pl.ds(head, 1), :] = lse

        @pl.when(head == heads - 1)
        def _():
            rest = lse_ref[0:heads, :]
            terms = []
            for _ in range(3):
                term = rest.astype(jnp.bfloat16).astype(jnp.float32)
                terms.append(term)
                rest = rest - term
            terms.append(jnp.zeros((16 - 3 * heads, SEQ_HALF), jnp.float32))
            o_ref[pl.ds(heads * HD, 16), :] = jnp.concatenate(terms, axis=0).astype(jnp.bfloat16)


def attention_cost(heads):
    return pl.CostEstimate(
        flops=heads * 4 * SEQ_HALF * SEQ_HALF * HD, bytes_accessed=2 * 1024 * 1024,
        transcendentals=heads * SEQ_HALF * SEQ_HALF)


def attend_own(where, chunk, q, kv):
    heads = GROUP // HD
    q_spec = pl.BlockSpec((ROWS, HD), lambda h, w: (0, heads * chunk + h))
    k_spec = pl.BlockSpec((ROWS, HD), lambda h, w: (0, h))
    v_spec = pl.BlockSpec((ROWS, HD), lambda h, w: (0, heads + h))
    return pl.pallas_call(
        own_kernel,
        grid_spec=pltpu.PrefetchScalarGridSpec(
            num_scalar_prefetch=1,
            grid=(heads,),
            in_specs=[q_spec] * 4 + [k_spec] * 4 + [v_spec] * 4,
            out_specs=[
                pl.BlockSpec((HD, SEQ_HALF), lambda h, w: (h, 0)),
                pl.BlockSpec((8, SEQ_HALF), lambda h, w: (0, 0)),
            ],
        ),
        out_shape=[
            jax.ShapeDtypeStruct((GROUP, SEQ_HALF), jnp.bfloat16),
            jax.ShapeDtypeStruct((8, SEQ_HALF), jnp.float32),
        ],
        compiler_params=pltpu.CompilerParams(vmem_limit_bytes=24 * 1024 * 1024),
        cost_estimate=attention_cost(heads),
        name="attend_own",
    )(where, *q, *kv, *kv)


def attend_far(where, at_half, q, kv, k_at, v_at):
    count = len(kv)
    heads = q.shape[1] // HD
    q_spec = pl.BlockSpec((SEQ_HALF, HD), lambda h, w: (0, h))
    k_spec = pl.BlockSpec((SEQ_HALF // count, HD), lambda h, w: (0, k_at + h))
    v_spec = pl.BlockSpec((SEQ_HALF // count, HD), lambda h, w: (0, v_at + h))
    return pl.pallas_call(
        functools.partial(far_kernel, at_half, heads),
        grid_spec=pltpu.PrefetchScalarGridSpec(
            num_scalar_prefetch=1,
            grid=(heads,),
            in_specs=[q_spec] + [k_spec] * count + [v_spec] * count,
            out_specs=pl.BlockSpec((heads * HD + 16, SEQ_HALF), lambda h, w: (0, 0)),
            scratch_shapes=[pltpu.VMEM((8, SEQ_HALF), jnp.float32)],
        ),
        out_shape=jax.ShapeDtypeStruct((heads * HD + 16, SEQ_HALF), jnp.bfloat16),
        compiler_params=pltpu.CompilerParams(vmem_limit_bytes=24 * 1024 * 1024),
        cost_estimate=attention_cost(heads),
        name="attend_far",
    )(where, q, *kv, *kv)


def merge_kernel(where_ref, own_ref, *refs):
    *far_refs, own_lse_ref, out_ref = refs
    late = where_ref[1] == 1
    at = 0
    for far_ref in far_refs:
        heads = far_ref.shape[0] // HD
        terms = far_ref[pl.ds(heads * HD, 16), :].astype(jnp.float32)
        far_lse = terms[0:heads] + terms[heads : 2 * heads] + terms[2 * heads : 3 * heads]
        far_lse = jnp.where(late, far_lse, -1e30)
        own_lse = own_lse_ref[at : at + heads, :]
        highest = jnp.maximum(own_lse, far_lse)
        own_part = jnp.exp2(own_lse - highest)
        far_part = jnp.exp2(far_lse - highest)
        total = own_part + far_part
        own_part = own_part / total
        far_part = far_part / total
        for head in range(heads):
            rows = pl.ds((at + head) * HD, HD)
            mixed = own_ref[rows, :].astype(jnp.float32) * own_part[head : head + 1]
            far = jnp.where(late, far_ref[pl.ds(head * HD, HD), :].astype(jnp.float32), 0.0)
            mixed = mixed + far * far_part[head : head + 1]
            out_ref[:, rows] = mixed.T.astype(jnp.bfloat16)
        at += heads


def merge(where, own, far, own_lse):
    whole = pl.BlockSpec(memory_space=pltpu.VMEM)
    return pl.pallas_call(
        merge_kernel,
        in_specs=[pl.BlockSpec(memory_space=pltpu.SMEM)] + [whole] * (len(far) + 2),
        out_specs=whole,
        out_shape=jax.ShapeDtypeStruct((SEQ_HALF, GROUP), jnp.bfloat16),
        compiler_params=pltpu.CompilerParams(vmem_limit_bytes=16 * 1024 * 1024),
        cost_estimate=pl.CostEstimate(flops=4 * 512 * 512, bytes_accessed=3 * 512 * 1024, transcendentals=0),
        name="merge_halves",
    )(where, own, *far, own_lse)


def norm_kernel(where_ref, *refs):
    own_refs, peer_refs = refs[0:2], refs[2:4]
    res_ref, gain_ref, bias_ref, out_ref = refs[4:8]
    core, x = where_ref[2], where_ref[3]
    blocks = []
    for half, parts in ((core, own_refs), (1 - core, peer_refs)):
        for apart, part, column in ((0, 0, 0), (-1, 0, 1), (1, 1, 0), (2, 1, 1)):
            at = ((x + apart) & 3) * (2 * BLOCK) + half * BLOCK
            at = pl.ds(pl.multiple_of(at, 128), BLOCK)
            added = parts[part][:, pl.ds(column * BLOCK, BLOCK)].astype(jnp.float32)
            blocks.append((at, deepnorm_alpha * res_ref[:, at].astype(jnp.float32) + added))
    mean = sum(jnp.sum(b, -1, keepdims=True) for _, b in blocks) / D
    blocks = [(at, b - mean) for at, b in blocks]
    var = sum(jnp.sum(b * b, -1, keepdims=True) for _, b in blocks) / D
    inv = lax.rsqrt(var + norm_eps)
    for at, b in blocks:
        out_ref[:, at] = (b * inv * gain_ref[:, at] + bias_ref[:, at]).astype(jnp.bfloat16)


def layer_norm(where, own, peer, residual, gain, bias):
    rows = 32
    part = pl.BlockSpec((rows, 2 * BLOCK), lambda i, w: (i, 0))
    full = pl.BlockSpec((rows, D), lambda i, w: (i, 0))
    vector = pl.BlockSpec((1, D), lambda i, w: (0, 0))
    return pl.pallas_call(
        norm_kernel,
        grid_spec=pltpu.PrefetchScalarGridSpec(
            num_scalar_prefetch=1,
            grid=(ROWS // rows,),
            in_specs=[part] * 4 + [full, vector, vector],
            out_specs=full,
        ),
        out_shape=jax.ShapeDtypeStruct((ROWS, D), jnp.bfloat16),
        compiler_params=pltpu.CompilerParams(vmem_limit_bytes=24 * 1024 * 1024),
        cost_estimate=pl.CostEstimate(flops=10 * ROWS * D, bytes_accessed=6 * ROWS * D, transcendentals=0),
        name="layer_norm",
    )(where, *own, *peer, residual, gain.reshape(1, D), bias.reshape(1, D))


def after(value, *others):
    return lax.optimization_barrier((value, *others))[0]


def columns_for(arrays, y, starts):
    return [
        jnp.concatenate(
            [lax.dynamic_slice_in_dim(a, s + ((y + step) & 3) * GROUP, GROUP, axis=1) for a, s in zip(arrays, starts)],
            axis=1,
        )
        for step in range(4)
    ]


def forward(part, step):
    return lax.ppermute(part, "y", ring(4, step))


def put(column, part, at):
    return lax.dynamic_update_slice(column, part[None], (at & 7, 0, 0))


def send(block, step):
    return lax.ppermute(block.astype(jnp.bfloat16), "y", ring(4, step))


def local(queries, keys, values, residual_in, out_weight, norm_gain, norm_bias):
    y = lax.axis_index("y")
    zh = lax.axis_index("zh")
    core = lax.axis_index("c")
    where = jnp.stack([y, zh, core, lax.axis_index("x")]).astype(jnp.int32)

    z = zh * 4 + lax.axis_index("zl")
    up_z = functools.partial(lax.ppermute, axis_name=("zl", "zh"), perm=z_ring(1))
    down_z = functools.partial(lax.ppermute, axis_name=("zl", "zh"), perm=z_ring(-1))

    shard = out_weight.T
    up = [shard, up_z(shard)]
    down = [shard, down_z(shard)]
    q = columns_for([queries, queries], y, [0, 2048])
    q = [q[0]] + [forward(q[s], s) for s in (1, 2, 3)]
    up.append(up_z(up[1]))
    down.append(down_z(down[1]))

    up[2], down[2], keys, values, *_ = lax.optimization_barrier((up[2], down[2], keys, values, *q))
    up.append(up_z(up[2]))
    down.append(down_z(down[2]))
    kv_1 = columns_for([keys, values], y, [2048, 2048])
    kv_1 = [kv_1[0]] + [forward(kv_1[s], s) for s in (1, 2, 3)]
    up.append(up_z(up[3]))

    q_first, q_next, q_last = (
        jnp.concatenate([b[:, start:end] for b in q], axis=0) for start, end in ((0, 512), (512, 768), (768, 1024))
    )
    last_kv = jnp.concatenate(
        [jnp.concatenate([b[:, at : at + PAIR] for b in kv_1], axis=0) for at in (PAIR, 3 * PAIR)], axis=1
    )
    q_first, last_kv, keys, values, *_ = lax.optimization_barrier(
        (q_first, last_kv, keys, values, up[4], down[3], *kv_1)
    )
    q_first = lax.ppermute(q_first, "zh", [(1, 0)])
    far_kv = lax.ppermute(last_kv, "zh", [(0, 1)])
    kv_0 = columns_for([keys, values], y, [0, 0])
    kv_0 = [kv_0[0]] + [forward(kv_0[s], s) for s in (1, 2, 3)]

    q_next = lax.ppermute(after(q_next, kv_0[1], kv_0[3]), "zh", [(1, 0)])

    weight = jnp.zeros((8, 224, GROUP), jnp.bfloat16)
    for step in range(5):
        weight = put(weight, up[step], z - step)
        if 0 < step < 4:
            weight = put(weight, down[step], z + step)
    weight = weight.reshape(2, 2, 2, 224, GROUP)
    mine = lax.dynamic_index_in_dim(weight, core, 1, keepdims=False)
    theirs = lax.ppermute(lax.dynamic_index_in_dim(weight, 1 - core, 1, keepdims=False), "c", ring(2, 1))
    first = jnp.where(core == 0, mine, theirs)
    second = jnp.where(core == 0, theirs, mine)
    weight = jnp.stack([first, second], axis=2).reshape(2, BLOCK, GROUP)
    left = [lax.ppermute(weight[0], "x", ring(4, 1))]
    right = [lax.ppermute(weight[0], "x", ring(4, -1))]
    rest = after(weight[1], left[0], right[0])
    left.append(lax.ppermute(rest, "x", ring(4, 1)))
    right.append(lax.ppermute(rest, "x", ring(4, -1)))
    far = jnp.stack([lax.ppermute(left[0], "x", ring(4, 1)), lax.ppermute(right[1], "x", ring(4, -1))])
    weights = [
        jnp.concatenate([weight, jnp.stack(left)], axis=1),
        jnp.concatenate([jnp.stack(right), far], axis=1),
    ]

    far_first = attend_far(where, 0, after(q_first, weight), kv_0, 0, 4)
    far_first = lax.ppermute(after(far_first, far_kv), "zh", [(0, 1)])
    far_last = attend_far(where, 1, q_last, [far_kv], 0, 2)
    own_0, lse_0 = attend_own(where, 0, q, kv_0)
    q[0], q_next = lax.optimization_barrier((q[0], q_next))
    own_1, lse_1 = attend_own(where, 1, q, kv_1)
    far_next = attend_far(where, 0, after(q_next, left[0], right[0]), kv_1, 0, 4)
    far_first = after(far_first, far_next)
    far_next = lax.ppermute(far_next, "zh", [(0, 1)])
    out_0 = merge(where, own_0, [far_first], lse_0)
    out_1 = merge(where, own_1, [far_next, far_last], lse_1)
    outs = [out_0, out_1]
    peers = [lax.ppermute(out, "c", ring(2, 1)) for out in outs]
    own, other = (
        [jnp.concatenate([part[s * ROWS : (s + 1) * ROWS] for part in parts], axis=1) for s in range(4)]
        for parts in (outs, peers)
    )

    sums = []
    peer_sums = []
    for weight in weights:

        def project(heads):
            return lax.dot_general(
                heads.reshape(ROWS, 2, GROUP), weight, (((1, 2), (0, 2)), ((), ())),
                preferred_element_type=jnp.float32,
            )

        up_1 = send(project(own[2]), 1)
        down_1 = send(project(other[2]), -1)
        up_2 = send(project(other[3]), 1)
        down_2 = send(project(own[1]), -1)
        up_3 = send(project(own[3]) + up_1.astype(jnp.float32), 1)
        down_3 = send(project(other[1]) + down_1.astype(jnp.float32), -1)
        total_other = project(other[0]) + up_2.astype(jnp.float32) + down_3.astype(jnp.float32)
        peer_sums.append(lax.ppermute(total_other.astype(jnp.bfloat16), "c", ring(2, 1)))
        total_own = project(own[0]) + down_2.astype(jnp.float32) + up_3.astype(jnp.float32)
        sums.append(total_own.astype(jnp.bfloat16))
        own[2], other[2], _, _ = lax.optimization_barrier((own[2], other[2], up_2, down_2))
        own[1], other[3], _, _ = lax.optimization_barrier((own[1], other[3], up_3, down_3))
    return layer_norm(where, sums, peer_sums, residual_in, norm_gain, norm_bias)


def solution(mesh):
    fine = Mesh(mesh.devices.reshape(4, 4, 2, 2, 4), AXES)
    tokens = P(AXES, None)
    in_specs = (tokens, tokens, tokens, tokens, P(("zh", "y"), ("x", "zl", "c")), P(), P())
    return jax.shard_map(local, mesh=fine, in_specs=in_specs, out_specs=tokens, check_vma=False)
```

```python
import functools
import math

import jax
import jax.numpy as jnp
from jax import lax
from jax.experimental import pallas as pl
from jax.experimental.pallas import tpu as pltpu
from jax.sharding import Mesh, PartitionSpec as P

HD = 128
GROUP = 512
ROWS = 128
SEQ_HALF = 512
PAIR = 2 * HD
D = 7168
HALF = D // 2
BLOCK = HALF // 4
FIRST = 512
REST = BLOCK - FIRST

deepnorm_alpha = 96.0**0.25
norm_eps = 1e-05
score_scale = math.log2(math.e) / math.sqrt(HD)

AXES = ("x", "zl", "c", "zh", "y")


def ring(n, step):
    return [(i, (i + step) % n) for i in range(n)]


def z_ring(step):
    pairs = []
    for z in range(8):
        to = (z + step) % 8
        pairs.append(((z % 4) * 2 + z // 4, (to % 4) * 2 + to // 4))
    return pairs


def softmax_part(q, k, v, keep):
    scores = lax.dot_general(k, q, (((1,), (1,)), ((), ())), preferred_element_type=jnp.float32)
    if keep is not None:
        scores = jnp.where(keep, scores, -1e30)
    highest = jnp.max(scores, axis=0, keepdims=True)
    expo = jnp.exp2((scores - highest) * score_scale)
    total = jnp.sum(expo, axis=0, keepdims=True)
    out = lax.dot_general(
        v, expo.astype(jnp.bfloat16), (((0,), (0,)), ((), ())), preferred_element_type=jnp.float32
    )
    return (out / total).astype(jnp.bfloat16), highest * score_scale + jnp.log2(total)


def own_kernel(where_ref, *refs):
    q_refs, k_refs, v_refs, o_ref, lse_ref = refs[0:4], refs[4:8], refs[8:12], refs[12], refs[13]
    head = pl.program_id(0)
    y = where_ref[0]
    q, k, v = (jnp.concatenate([r[...] for r in part], axis=0) for part in (q_refs, k_refs, v_refs))

    def position(axis):
        at = lax.broadcasted_iota(jnp.int32, (SEQ_HALF, SEQ_HALF), axis)
        return ((y - at // ROWS) & 3) * ROWS + (at & (ROWS - 1))

    out, lse = softmax_part(q, k, v, position(0) <= position(1))
    o_ref[...] = out
    lse_ref[pl.ds(head, 1), :] = lse


def far_kernel(at_half, heads, where_ref, q_ref, *refs):
    *kv_refs, o_ref, lse_ref = refs
    count = len(kv_refs) // 2
    k_refs, v_refs = kv_refs[:count], kv_refs[count:]
    head = pl.program_id(0)

    @pl.when(where_ref[1] == at_half)
    def _():
        k, v = (jnp.concatenate([r[...] for r in part], axis=0) for part in (k_refs, v_refs))
        out, lse = softmax_part(q_ref[...], k, v, None)
        o_ref[pl.ds(pl.multiple_of(head * HD, HD), HD), :] = out
        lse_ref[pl.ds(head, 1), :] = lse

        @pl.when(head == heads - 1)
        def _():
            rest = lse_ref[0:heads, :]
            terms = []
            for _ in range(3):
                term = rest.astype(jnp.bfloat16).astype(jnp.float32)
                terms.append(term)
                rest = rest - term
            terms.append(jnp.zeros((16 - 3 * heads, SEQ_HALF), jnp.float32))
            o_ref[pl.ds(heads * HD, 16), :] = jnp.concatenate(terms, axis=0).astype(jnp.bfloat16)


def attention_cost(heads):
    return pl.CostEstimate(
        flops=heads * 4 * SEQ_HALF * SEQ_HALF * HD, bytes_accessed=2 * 1024 * 1024,
        transcendentals=heads * SEQ_HALF * SEQ_HALF)


def attend_own(where, chunk, q, kv):
    heads = GROUP // HD
    q_spec = pl.BlockSpec((ROWS, HD), lambda h, w: (0, heads * chunk + h))
    k_spec = pl.BlockSpec((ROWS, HD), lambda h, w: (0, h))
    v_spec = pl.BlockSpec((ROWS, HD), lambda h, w: (0, heads + h))
    return pl.pallas_call(
        own_kernel,
        grid_spec=pltpu.PrefetchScalarGridSpec(
            num_scalar_prefetch=1,
            grid=(heads,),
            in_specs=[q_spec] * 4 + [k_spec] * 4 + [v_spec] * 4,
            out_specs=[
                pl.BlockSpec((HD, SEQ_HALF), lambda h, w: (h, 0)),
                pl.BlockSpec((8, SEQ_HALF), lambda h, w: (0, 0)),
            ],
        ),
        out_shape=[
            jax.ShapeDtypeStruct((GROUP, SEQ_HALF), jnp.bfloat16),
            jax.ShapeDtypeStruct((8, SEQ_HALF), jnp.float32),
        ],
        compiler_params=pltpu.CompilerParams(vmem_limit_bytes=24 * 1024 * 1024),
        cost_estimate=attention_cost(heads),
        name="attend_own",
    )(where, *q, *kv, *kv)


def attend_far(where, at_half, q, kv, k_at, v_at):
    count = len(kv)
    heads = q.shape[1] // HD
    q_spec = pl.BlockSpec((SEQ_HALF, HD), lambda h, w: (0, h))
    k_spec = pl.BlockSpec((SEQ_HALF // count, HD), lambda h, w: (0, k_at + h))
    v_spec = pl.BlockSpec((SEQ_HALF // count, HD), lambda h, w: (0, v_at + h))
    return pl.pallas_call(
        functools.partial(far_kernel, at_half, heads),
        grid_spec=pltpu.PrefetchScalarGridSpec(
            num_scalar_prefetch=1,
            grid=(heads,),
            in_specs=[q_spec] + [k_spec] * count + [v_spec] * count,
            out_specs=pl.BlockSpec((heads * HD + 16, SEQ_HALF), lambda h, w: (0, 0)),
            scratch_shapes=[pltpu.VMEM((8, SEQ_HALF), jnp.float32)],
        ),
        out_shape=jax.ShapeDtypeStruct((heads * HD + 16, SEQ_HALF), jnp.bfloat16),
        compiler_params=pltpu.CompilerParams(vmem_limit_bytes=24 * 1024 * 1024),
        cost_estimate=attention_cost(heads),
        name="attend_far",
    )(where, q, *kv, *kv)


def merge_kernel(where_ref, own_ref, *refs):
    *far_refs, own_lse_ref, out_ref = refs
    late = where_ref[1] == 1
    at = 0
    for far_ref in far_refs:
        heads = far_ref.shape[0] // HD
        terms = far_ref[pl.ds(heads * HD, 16), :].astype(jnp.float32)
        far_lse = terms[0:heads] + terms[heads : 2 * heads] + terms[2 * heads : 3 * heads]
        far_lse = jnp.where(late, far_lse, -1e30)
        own_lse = own_lse_ref[at : at + heads, :]
        highest = jnp.maximum(own_lse, far_lse)
        own_part = jnp.exp2(own_lse - highest)
        far_part = jnp.exp2(far_lse - highest)
        total = own_part + far_part
        own_part = own_part / total
        far_part = far_part / total
        for head in range(heads):
            rows = pl.ds((at + head) * HD, HD)
            mixed = own_ref[rows, :].astype(jnp.float32) * own_part[head : head + 1]
            far = jnp.where(late, far_ref[pl.ds(head * HD, HD), :].astype(jnp.float32), 0.0)
            mixed = mixed + far * far_part[head : head + 1]
            out_ref[:, rows] = mixed.T.astype(jnp.bfloat16)
        at += heads


def merge(where, own, far, own_lse):
    whole = pl.BlockSpec(memory_space=pltpu.VMEM)
    return pl.pallas_call(
        merge_kernel,
        in_specs=[pl.BlockSpec(memory_space=pltpu.SMEM)] + [whole] * (len(far) + 2),
        out_specs=whole,
        out_shape=jax.ShapeDtypeStruct((SEQ_HALF, GROUP), jnp.bfloat16),
        compiler_params=pltpu.CompilerParams(vmem_limit_bytes=16 * 1024 * 1024),
        cost_estimate=pl.CostEstimate(flops=4 * 512 * 512, bytes_accessed=3 * 512 * 1024, transcendentals=0),
        name="merge_halves",
    )(where, own, *far, own_lse)


PLACES = (
    (0, 0, BLOCK, 0, 0),
    (-1, 0, FIRST, 0, BLOCK),
    (1, 0, FIRST, 0, BLOCK + FIRST),
    (-1, FIRST, REST, 1, 0),
    (1, FIRST, REST, 1, REST),
    (2, 0, BLOCK, 1, 2 * REST),
)


def norm_kernel(where_ref, *refs):
    own_refs, peer_refs = refs[0:2], refs[2:4]
    res_ref, gain_ref, bias_ref, out_ref = refs[4:8]
    core, x = where_ref[2], where_ref[3]
    blocks = []
    for half, parts in ((core, own_refs), (1 - core, peer_refs)):
        for apart, start, width, part, column in PLACES:
            at = ((x + apart) & 3) * (2 * BLOCK) + half * BLOCK + start
            at = pl.ds(pl.multiple_of(at, 128), width)
            added = parts[part][:, pl.ds(column, width)].astype(jnp.float32)
            blocks.append((at, deepnorm_alpha * res_ref[:, at].astype(jnp.float32) + added))
    mean = sum(jnp.sum(b, -1, keepdims=True) for _, b in blocks) / D
    blocks = [(at, b - mean) for at, b in blocks]
    var = sum(jnp.sum(b * b, -1, keepdims=True) for _, b in blocks) / D
    inv = lax.rsqrt(var + norm_eps)
    for at, b in blocks:
        out_ref[:, at] = (b * inv * gain_ref[:, at] + bias_ref[:, at]).astype(jnp.bfloat16)


def layer_norm(where, own, peer, residual, gain, bias):
    rows = 32
    parts = [pl.BlockSpec((rows, BLOCK + 2 * width), lambda i, w: (i, 0)) for width in (FIRST, REST)]
    full = pl.BlockSpec((rows, D), lambda i, w: (i, 0))
    vector = pl.BlockSpec((1, D), lambda i, w: (0, 0))
    return pl.pallas_call(
        norm_kernel,
        grid_spec=pltpu.PrefetchScalarGridSpec(
            num_scalar_prefetch=1,
            grid=(ROWS // rows,),
            in_specs=parts * 2 + [full, vector, vector],
            out_specs=full,
        ),
        out_shape=jax.ShapeDtypeStruct((ROWS, D), jnp.bfloat16),
        compiler_params=pltpu.CompilerParams(vmem_limit_bytes=24 * 1024 * 1024),
        cost_estimate=pl.CostEstimate(flops=10 * ROWS * D, bytes_accessed=6 * ROWS * D, transcendentals=0),
        name="layer_norm",
    )(where, *own, *peer, residual, gain.reshape(1, D), bias.reshape(1, D))


def after(value, *others):
    return lax.optimization_barrier((value, *others))[0]


def columns_for(arrays, y, starts):
    return [
        jnp.concatenate(
            [lax.dynamic_slice_in_dim(a, s + ((y + step) & 3) * GROUP, GROUP, axis=1) for a, s in zip(arrays, starts)],
            axis=1,
        )
        for step in range(4)
    ]


def forward(part, step):
    return lax.ppermute(part, "y", ring(4, step))


def put(column, part, at):
    return lax.dynamic_update_slice(column, part[None], (at & 7, 0, 0))


def send(block, step):
    return lax.ppermute(block.astype(jnp.bfloat16), "y", ring(4, step))


def local(queries, keys, values, residual_in, out_weight, norm_gain, norm_bias):
    y = lax.axis_index("y")
    zh = lax.axis_index("zh")
    core = lax.axis_index("c")
    where = jnp.stack([y, zh, core, lax.axis_index("x")]).astype(jnp.int32)

    z = zh * 4 + lax.axis_index("zl")
    up_z = functools.partial(lax.ppermute, axis_name=("zl", "zh"), perm=z_ring(1))
    down_z = functools.partial(lax.ppermute, axis_name=("zl", "zh"), perm=z_ring(-1))

    shard = out_weight.T
    up = [shard, up_z(shard)]
    down = [shard, down_z(shard)]
    q = columns_for([queries, queries], y, [0, 2048])
    q = [q[0]] + [forward(q[s], s) for s in (1, 2, 3)]
    up.append(up_z(up[1]))
    down.append(down_z(down[1]))

    up[2], down[2], keys, values, *_ = lax.optimization_barrier((up[2], down[2], keys, values, *q))
    up.append(up_z(up[2]))
    down.append(down_z(down[2]))
    kv_1 = columns_for([keys, values], y, [2048, 2048])
    kv_1 = [kv_1[0]] + [forward(kv_1[s], s) for s in (1, 2, 3)]
    up.append(up_z(up[3]))

    q_first, q_next, q_last = (
        jnp.concatenate([b[:, start:end] for b in q], axis=0) for start, end in ((0, 512), (512, 768), (768, 1024))
    )
    last_kv = jnp.concatenate(
        [jnp.concatenate([b[:, at : at + PAIR] for b in kv_1], axis=0) for at in (PAIR, 3 * PAIR)], axis=1
    )
    q_first, last_kv, keys, values, *_ = lax.optimization_barrier(
        (q_first, last_kv, keys, values, up[4], down[3], *kv_1)
    )
    q_first = lax.ppermute(q_first, "zh", [(1, 0)])
    far_kv = lax.ppermute(last_kv, "zh", [(0, 1)])
    kv_0 = columns_for([keys, values], y, [0, 0])
    kv_0 = [kv_0[0]] + [forward(kv_0[s], s) for s in (1, 2, 3)]

    q_next = lax.ppermute(after(q_next, kv_0[1], kv_0[3]), "zh", [(1, 0)])

    weight = jnp.zeros((8, 224, GROUP), jnp.bfloat16)
    for step in range(5):
        weight = put(weight, up[step], z - step)
        if 0 < step < 4:
            weight = put(weight, down[step], z + step)
    weight = weight.reshape(2, 2, 2, 224, GROUP)
    mine = lax.dynamic_index_in_dim(weight, core, 1, keepdims=False)
    theirs = lax.ppermute(lax.dynamic_index_in_dim(weight, 1 - core, 1, keepdims=False), "c", ring(2, 1))
    first = jnp.where(core == 0, mine, theirs)
    second = jnp.where(core == 0, theirs, mine)
    weight = jnp.stack([first, second], axis=2).reshape(2, BLOCK, GROUP)
    first, rest = weight[:, :FIRST], weight[:, FIRST:]
    left = [lax.ppermute(first, "x", ring(4, 1))]
    right = [lax.ppermute(first, "x", ring(4, -1))]
    rest = after(rest, left[0], right[0])
    left.append(lax.ppermute(rest, "x", ring(4, 1)))
    right.append(lax.ppermute(rest, "x", ring(4, -1)))
    weights = [jnp.concatenate([weight, left[0], right[0]], axis=1)]

    far_first = attend_far(where, 0, after(q_first, weight), kv_0, 0, 4)
    far_first = lax.ppermute(after(far_first, far_kv), "zh", [(0, 1)])
    far_last = attend_far(where, 1, q_last, [far_kv], 0, 2)
    own_0, lse_0 = attend_own(where, 0, q, kv_0)
    own_1, lse_1 = attend_own(where, 1, q, kv_1)
    far_next = attend_far(where, 0, after(q_next, left[0], right[0], own_0, own_1, far_last), kv_1, 0, 4)
    far_first = after(far_first, far_next)
    far_next = lax.ppermute(far_next, "zh", [(0, 1)])
    out_0 = merge(where, own_0, [far_first], lse_0)
    out_1 = merge(where, own_1, [far_next, far_last], lse_1)
    outs = [out_0, out_1]
    peers = [lax.ppermute(out, "c", ring(2, 1)) for out in outs]
    own, other = (
        [jnp.concatenate([part[s * ROWS : (s + 1) * ROWS] for part in parts], axis=1) for s in range(4)]
        for parts in (outs, peers)
    )

    *heads, _ = lax.optimization_barrier((*own, *other, peers[1]))
    own, other = heads[:4], heads[4:]

    sums = []
    peer_sums = []
    for weight in weights:

        def project(heads):
            return lax.dot_general(
                heads.reshape(ROWS, 2, GROUP), weight, (((1, 2), (0, 2)), ((), ())),
                preferred_element_type=jnp.float32,
            )

        up_1 = send(project(own[2]), 1)
        down_1 = send(project(other[2]), -1)
        if len(weights) == 1:
            near, right[1], _, _ = lax.optimization_barrier((left[0], right[1], up_1, down_1))
            far = [lax.ppermute(near, "x", ring(4, 1)), lax.ppermute(right[1], "x", ring(4, -1))]
            weights.append(jnp.concatenate([left[1], right[1], *far], axis=1))
        up_2 = send(project(other[3]), 1)
        down_2 = send(project(own[1]), -1)
        up_3 = send(project(own[3]) + up_1.astype(jnp.float32), 1)
        down_3 = send(project(other[1]) + down_1.astype(jnp.float32), -1)
        total_other = project(other[0]) + up_2.astype(jnp.float32) + down_3.astype(jnp.float32)
        peer_sums.append(lax.ppermute(total_other.astype(jnp.bfloat16), "c", ring(2, 1)))
        total_own = project(own[0]) + down_2.astype(jnp.float32) + up_3.astype(jnp.float32)
        sums.append(total_own.astype(jnp.bfloat16))
        own[2], other[2], _, _ = lax.optimization_barrier((own[2], other[2], up_2, down_2))
        own[1], other[3], _, _ = lax.optimization_barrier((own[1], other[3], up_3, down_3))
    return layer_norm(where, sums, peer_sums, residual_in, norm_gain, norm_bias)


def solution(mesh):
    fine = Mesh(mesh.devices.reshape(4, 4, 2, 2, 4), AXES)
    tokens = P(AXES, None)
    in_specs = (tokens, tokens, tokens, tokens, P(("zh", "y"), ("x", "zl", "c")), P(), P())
    return jax.shard_map(local, mesh=fine, in_specs=in_specs, out_specs=tokens, check_vma=False)
```

```python
import functools
import math

import jax
import jax.numpy as jnp
from jax import lax
from jax.experimental import pallas as pl
from jax.experimental.pallas import tpu as pltpu
from jax.sharding import Mesh, PartitionSpec as P

HD = 128
GROUP = 512
ROWS = 128
SEQ_HALF = 512
PAIR = 2 * HD
D = 7168
HALF = D // 2
BLOCK = HALF // 4
FIRST = 512
REST = BLOCK - FIRST

deepnorm_alpha = 96.0**0.25
norm_eps = 1e-05
score_scale = math.log2(math.e) / math.sqrt(HD)

AXES = ("x", "zl", "c", "zh", "y")


def ring(n, step):
    return [(i, (i + step) % n) for i in range(n)]


def z_ring(step):
    pairs = []
    for z in range(8):
        to = (z + step) % 8
        pairs.append(((z % 4) * 2 + z // 4, (to % 4) * 2 + to // 4))
    return pairs


def softmax_part(q, k, v, keep):
    scores = lax.dot_general(k, q, (((1,), (1,)), ((), ())), preferred_element_type=jnp.float32)
    if keep is not None:
        scores = jnp.where(keep, scores, -1e30)
    highest = jnp.max(scores, axis=0, keepdims=True)
    expo = jnp.exp2((scores - highest) * score_scale)
    total = jnp.sum(expo, axis=0, keepdims=True)
    out = lax.dot_general(
        v, expo.astype(jnp.bfloat16), (((0,), (0,)), ((), ())), preferred_element_type=jnp.float32
    )
    return (out / total).astype(jnp.bfloat16), highest * score_scale + jnp.log2(total)


def own_kernel(where_ref, *refs):
    q_refs, k_refs, v_refs, o_ref, lse_ref = refs[0:4], refs[4:8], refs[8:12], refs[12], refs[13]
    head = pl.program_id(0)
    y = where_ref[0]
    q, k, v = (jnp.concatenate([r[...] for r in part], axis=0) for part in (q_refs, k_refs, v_refs))

    def position(axis):
        at = lax.broadcasted_iota(jnp.int32, (SEQ_HALF, SEQ_HALF), axis)
        return ((y - at // ROWS) & 3) * ROWS + (at & (ROWS - 1))

    out, lse = softmax_part(q, k, v, position(0) <= position(1))
    o_ref[...] = out
    lse_ref[pl.ds(head, 1), :] = lse


def far_kernel(at_half, heads, where_ref, q_ref, *refs):
    *kv_refs, o_ref, lse_ref = refs
    count = len(kv_refs) // 2
    k_refs, v_refs = kv_refs[:count], kv_refs[count:]
    head = pl.program_id(0)

    @pl.when(where_ref[1] == at_half)
    def _():
        k, v = (jnp.concatenate([r[...] for r in part], axis=0) for part in (k_refs, v_refs))
        out, lse = softmax_part(q_ref[...], k, v, None)
        o_ref[pl.ds(pl.multiple_of(head * HD, HD), HD), :] = out
        lse_ref[pl.ds(head, 1), :] = lse

        @pl.when(head == heads - 1)
        def _():
            rest = lse_ref[0:heads, :]
            terms = []
            for _ in range(3):
                term = rest.astype(jnp.bfloat16).astype(jnp.float32)
                terms.append(term)
                rest = rest - term
            terms.append(jnp.zeros((16 - 3 * heads, SEQ_HALF), jnp.float32))
            o_ref[pl.ds(heads * HD, 16), :] = jnp.concatenate(terms, axis=0).astype(jnp.bfloat16)


def attention_cost(heads):
    return pl.CostEstimate(
        flops=heads * 4 * SEQ_HALF * SEQ_HALF * HD, bytes_accessed=2 * 1024 * 1024,
        transcendentals=heads * SEQ_HALF * SEQ_HALF)


def attend_own(where, chunk, q, kv):
    heads = GROUP // HD
    q_spec = pl.BlockSpec((ROWS, HD), lambda h, w: (0, heads * chunk + h))
    k_spec = pl.BlockSpec((ROWS, HD), lambda h, w: (0, h))
    v_spec = pl.BlockSpec((ROWS, HD), lambda h, w: (0, heads + h))
    return pl.pallas_call(
        own_kernel,
        grid_spec=pltpu.PrefetchScalarGridSpec(
            num_scalar_prefetch=1,
            grid=(heads,),
            in_specs=[q_spec] * 4 + [k_spec] * 4 + [v_spec] * 4,
            out_specs=[
                pl.BlockSpec((HD, SEQ_HALF), lambda h, w: (h, 0)),
                pl.BlockSpec((8, SEQ_HALF), lambda h, w: (0, 0)),
            ],
        ),
        out_shape=[
            jax.ShapeDtypeStruct((GROUP, SEQ_HALF), jnp.bfloat16),
            jax.ShapeDtypeStruct((8, SEQ_HALF), jnp.float32),
        ],
        compiler_params=pltpu.CompilerParams(vmem_limit_bytes=24 * 1024 * 1024),
        cost_estimate=attention_cost(heads),
        name="attend_own",
    )(where, *q, *kv, *kv)


def attend_far(where, at_half, q, kv, k_at, v_at):
    count = len(kv)
    heads = q.shape[1] // HD
    q_spec = pl.BlockSpec((SEQ_HALF, HD), lambda h, w: (0, h))
    k_spec = pl.BlockSpec((SEQ_HALF // count, HD), lambda h, w: (0, k_at + h))
    v_spec = pl.BlockSpec((SEQ_HALF // count, HD), lambda h, w: (0, v_at + h))
    return pl.pallas_call(
        functools.partial(far_kernel, at_half, heads),
        grid_spec=pltpu.PrefetchScalarGridSpec(
            num_scalar_prefetch=1,
            grid=(heads,),
            in_specs=[q_spec] + [k_spec] * count + [v_spec] * count,
            out_specs=pl.BlockSpec((heads * HD + 16, SEQ_HALF), lambda h, w: (0, 0)),
            scratch_shapes=[pltpu.VMEM((8, SEQ_HALF), jnp.float32)],
        ),
        out_shape=jax.ShapeDtypeStruct((heads * HD + 16, SEQ_HALF), jnp.bfloat16),
        compiler_params=pltpu.CompilerParams(vmem_limit_bytes=24 * 1024 * 1024),
        cost_estimate=attention_cost(heads),
        name="attend_far",
    )(where, q, *kv, *kv)


def merge_kernel(where_ref, own_ref, *refs):
    *far_refs, own_lse_ref, out_ref = refs
    late = where_ref[1] == 1
    at = 0
    for far_ref in far_refs:
        heads = far_ref.shape[0] // HD
        terms = far_ref[pl.ds(heads * HD, 16), :].astype(jnp.float32)
        far_lse = terms[0:heads] + terms[heads : 2 * heads] + terms[2 * heads : 3 * heads]
        far_lse = jnp.where(late, far_lse, -1e30)
        own_lse = own_lse_ref[at : at + heads, :]
        highest = jnp.maximum(own_lse, far_lse)
        own_part = jnp.exp2(own_lse - highest)
        far_part = jnp.exp2(far_lse - highest)
        total = own_part + far_part
        own_part = own_part / total
        far_part = far_part / total
        for head in range(heads):
            rows = pl.ds((at + head) * HD, HD)
            mixed = own_ref[rows, :].astype(jnp.float32) * own_part[head : head + 1]
            far = jnp.where(late, far_ref[pl.ds(head * HD, HD), :].astype(jnp.float32), 0.0)
            mixed = mixed + far * far_part[head : head + 1]
            out_ref[:, rows] = mixed.T.astype(jnp.bfloat16)
        at += heads


def merge(where, own, far, own_lse):
    whole = pl.BlockSpec(memory_space=pltpu.VMEM)
    return pl.pallas_call(
        merge_kernel,
        in_specs=[pl.BlockSpec(memory_space=pltpu.SMEM)] + [whole] * (len(far) + 2),
        out_specs=whole,
        out_shape=jax.ShapeDtypeStruct((SEQ_HALF, GROUP), jnp.bfloat16),
        compiler_params=pltpu.CompilerParams(vmem_limit_bytes=16 * 1024 * 1024),
        cost_estimate=pl.CostEstimate(flops=4 * 512 * 512, bytes_accessed=3 * 512 * 1024, transcendentals=0),
        name="merge_halves",
    )(where, own, *far, own_lse)


def norm_kernel(where_ref, *refs):
    own_refs, peer_refs = refs[0:2], refs[2:4]
    res_ref, gain_ref, bias_ref, out_ref = refs[4:8]
    core = where_ref[2]
    blocks = []
    for half, parts in ((core, own_refs), (1 - core, peer_refs)):
        for x in range(4):
            for part, start, width in ((0, 0, FIRST), (1, FIRST, REST)):
                at = x * (2 * BLOCK) + half * BLOCK + start
                at = pl.ds(pl.multiple_of(at, 128), width)
                added = parts[part][:, pl.ds(x * width, width)].astype(jnp.float32)
                blocks.append((at, deepnorm_alpha * res_ref[:, at].astype(jnp.float32) + added))
    mean = sum(jnp.sum(b, -1, keepdims=True) for _, b in blocks) / D
    blocks = [(at, b - mean) for at, b in blocks]
    var = sum(jnp.sum(b * b, -1, keepdims=True) for _, b in blocks) / D
    inv = lax.rsqrt(var + norm_eps)
    for at, b in blocks:
        out_ref[:, at] = (b * inv * gain_ref[:, at] + bias_ref[:, at]).astype(jnp.bfloat16)


def layer_norm(where, own, peer, residual, gain, bias):
    rows = 32
    parts = [pl.BlockSpec((rows, 4 * width), lambda i, w: (i, 0)) for width in (FIRST, REST)]
    full = pl.BlockSpec((rows, D), lambda i, w: (i, 0))
    vector = pl.BlockSpec((1, D), lambda i, w: (0, 0))
    return pl.pallas_call(
        norm_kernel,
        grid_spec=pltpu.PrefetchScalarGridSpec(
            num_scalar_prefetch=1,
            grid=(ROWS // rows,),
            in_specs=parts * 2 + [full, vector, vector],
            out_specs=full,
        ),
        out_shape=jax.ShapeDtypeStruct((ROWS, D), jnp.bfloat16),
        compiler_params=pltpu.CompilerParams(vmem_limit_bytes=24 * 1024 * 1024),
        cost_estimate=pl.CostEstimate(flops=10 * ROWS * D, bytes_accessed=6 * ROWS * D, transcendentals=0),
        name="layer_norm",
    )(where, *own, *peer, residual, gain.reshape(1, D), bias.reshape(1, D))


def after(value, *others):
    return lax.optimization_barrier((value, *others))[0]


def columns_for(arrays, y, starts):
    return [
        jnp.concatenate(
            [lax.dynamic_slice_in_dim(a, s + ((y + step) & 3) * GROUP, GROUP, axis=1) for a, s in zip(arrays, starts)],
            axis=1,
        )
        for step in range(4)
    ]


def forward(part, step):
    return lax.ppermute(part, "y", ring(4, step))


def put(column, part, at):
    return lax.dynamic_update_slice(column, part[None], (at & 7, 0, 0))


def send(block, step):
    return lax.ppermute(block.astype(jnp.bfloat16), "y", ring(4, step))


def local(queries, keys, values, residual_in, out_weight, norm_gain, norm_bias):
    y = lax.axis_index("y")
    zh = lax.axis_index("zh")
    core = lax.axis_index("c")
    where = jnp.stack([y, zh, core]).astype(jnp.int32)

    z = zh * 4 + lax.axis_index("zl")
    up_z = functools.partial(lax.ppermute, axis_name=("zl", "zh"), perm=z_ring(1))
    down_z = functools.partial(lax.ppermute, axis_name=("zl", "zh"), perm=z_ring(-1))

    shard = out_weight.T
    up = [shard, up_z(shard)]
    down = [shard, down_z(shard)]
    q = columns_for([queries, queries], y, [0, 2048])
    q = [q[0]] + [forward(q[s], s) for s in (1, 2, 3)]
    up.append(up_z(up[1]))
    down.append(down_z(down[1]))

    up[2], down[2], keys, values, *_ = lax.optimization_barrier((up[2], down[2], keys, values, *q))
    up.append(up_z(up[2]))
    down.append(down_z(down[2]))
    kv_1 = columns_for([keys, values], y, [2048, 2048])
    kv_1 = [kv_1[0]] + [forward(kv_1[s], s) for s in (1, 2, 3)]
    up.append(up_z(up[3]))

    q_first, q_next, q_last = (
        jnp.concatenate([b[:, start:end] for b in q], axis=0) for start, end in ((0, 512), (512, 768), (768, 1024))
    )
    last_kv = jnp.concatenate(
        [jnp.concatenate([b[:, at : at + PAIR] for b in kv_1], axis=0) for at in (PAIR, 3 * PAIR)], axis=1
    )
    q_first, last_kv, keys, values, *_ = lax.optimization_barrier(
        (q_first, last_kv, keys, values, up[4], down[3], *kv_1)
    )
    q_first = lax.ppermute(q_first, "zh", [(1, 0)])
    far_kv = lax.ppermute(last_kv, "zh", [(0, 1)])
    kv_0 = columns_for([keys, values], y, [0, 0])
    kv_0 = [kv_0[0]] + [forward(kv_0[s], s) for s in (1, 2, 3)]

    q_next = lax.ppermute(after(q_next, kv_0[1], kv_0[3]), "zh", [(1, 0)])

    weight = jnp.zeros((8, 224, GROUP), jnp.bfloat16)
    for step in range(5):
        weight = put(weight, up[step], z - step)
        if 0 < step < 4:
            weight = put(weight, down[step], z + step)
    weight = weight.reshape(2, 2, 2, 224, GROUP)
    mine = lax.dynamic_index_in_dim(weight, core, 1, keepdims=False)
    theirs = after(lax.dynamic_index_in_dim(weight, 1 - core, 1, keepdims=False), *kv_1[1:])
    theirs = lax.ppermute(theirs, "c", ring(2, 1))
    first = jnp.where(core == 0, mine, theirs)
    second = jnp.where(core == 0, theirs, mine)
    weight = jnp.stack([first, second], axis=2).reshape(2, BLOCK, GROUP)
    rest = after(weight[:, FIRST:], q_first, *kv_0[1:])
    weights = [lax.all_gather(part, "x", axis=1, tiled=True) for part in (weight[:, :FIRST], rest)]

    far_first = attend_far(where, 0, after(q_first, weight), kv_0, 0, 4)
    q[0] = after(q[0], far_first)
    far_first = lax.ppermute(after(far_first, far_kv), "zh", [(0, 1)])
    far_last = attend_far(where, 1, q_last, [far_kv], 0, 2)
    own_0, lse_0 = attend_own(where, 0, q, kv_0)
    own_1, lse_1 = attend_own(where, 1, q, kv_1)
    far_next = attend_far(where, 0, after(q_next, own_0, own_1, far_last), kv_1, 0, 4)
    far_first = after(far_first, far_next)
    far_next = lax.ppermute(far_next, "zh", [(0, 1)])
    out_0 = merge(where, own_0, [far_first], lse_0)
    out_1 = merge(where, after(own_1, out_0), [far_next, far_last], lse_1)
    outs = [out_0, out_1]
    peers = [lax.ppermute(out, "c", ring(2, 1)) for out in outs]
    own, other = (
        [jnp.concatenate([part[s * ROWS : (s + 1) * ROWS] for part in parts], axis=1) for s in range(4)]
        for parts in (outs, peers)
    )

    *heads, _ = lax.optimization_barrier((*own, *other, peers[1]))
    own, other = heads[:4], heads[4:]

    sums = []
    peer_sums = []
    for weight in weights:

        def project(heads):
            return lax.dot_general(
                heads.reshape(ROWS, 2, GROUP), weight, (((1, 2), (0, 2)), ((), ())),
                preferred_element_type=jnp.float32,
            )

        up_1 = send(project(own[2]), 1)
        down_1 = send(project(other[2]), -1)
        up_2 = send(project(other[3]), 1)
        down_2 = send(project(own[1]), -1)
        up_3 = send(project(own[3]) + up_1.astype(jnp.float32), 1)
        down_3 = send(project(other[1]) + down_1.astype(jnp.float32), -1)
        total_other = project(other[0]) + up_2.astype(jnp.float32) + down_3.astype(jnp.float32)
        peer_sums.append(lax.ppermute(total_other.astype(jnp.bfloat16), "c", ring(2, 1)))
        total_own = project(own[0]) + down_2.astype(jnp.float32) + up_3.astype(jnp.float32)
        sums.append(total_own.astype(jnp.bfloat16))
        own[2], other[2], _, _ = lax.optimization_barrier((own[2], other[2], up_2, down_2))
        own[1], other[3], _, _ = lax.optimization_barrier((own[1], other[3], up_3, down_3))
    return layer_norm(where, sums, peer_sums, residual_in, norm_gain, norm_bias)


def solution(mesh):
    fine = Mesh(mesh.devices.reshape(4, 4, 2, 2, 4), AXES)
    tokens = P(AXES, None)
    in_specs = (tokens, tokens, tokens, tokens, P(("zh", "y"), ("x", "zl", "c")), P(), P())
    return jax.shard_map(local, mesh=fine, in_specs=in_specs, out_specs=tokens, check_vma=False)
```

```python
import functools
import math

import jax
import jax.numpy as jnp
from jax import lax
from jax.experimental import pallas as pl
from jax.experimental.pallas import tpu as pltpu
from jax.sharding import Mesh, PartitionSpec as P

HD = 128
GROUP = 512
ROWS = 128
SEQ_HALF = 512
PAIR = 2 * HD
D = 7168
HALF = D // 2
BLOCK = HALF // 4

deepnorm_alpha = 96.0**0.25
norm_eps = 1e-05
score_scale = math.log2(math.e) / math.sqrt(HD)

AXES = ("x", "zl", "c", "zh", "y")


def ring(n, step):
    return [(i, (i + step) % n) for i in range(n)]


def z_ring(step):
    pairs = []
    for z in range(8):
        to = (z + step) % 8
        pairs.append(((z % 4) * 2 + z // 4, (to % 4) * 2 + to // 4))
    return pairs


def softmax_part(q, k, v, keep):
    scores = lax.dot_general(k, q, (((1,), (1,)), ((), ())), preferred_element_type=jnp.float32)
    if keep is not None:
        scores = jnp.where(keep, scores, -1e30)
    highest = jnp.max(scores, axis=0, keepdims=True)
    expo = jnp.exp2((scores - highest) * score_scale)
    total = jnp.sum(expo, axis=0, keepdims=True)
    out = lax.dot_general(
        v, expo.astype(jnp.bfloat16), (((0,), (0,)), ((), ())), preferred_element_type=jnp.float32
    )
    return (out / total).astype(jnp.bfloat16), highest * score_scale + jnp.log2(total)


def own_kernel(where_ref, *refs):
    q_refs, k_refs, v_refs, o_ref, lse_ref = refs[0:4], refs[4:8], refs[8:12], refs[12], refs[13]
    head = pl.program_id(0)
    y = where_ref[0]
    q, k, v = (jnp.concatenate([r[...] for r in part], axis=0) for part in (q_refs, k_refs, v_refs))

    def position(axis):
        at = lax.broadcasted_iota(jnp.int32, (SEQ_HALF, SEQ_HALF), axis)
        return ((y - at // ROWS) & 3) * ROWS + (at & (ROWS - 1))

    out, lse = softmax_part(q, k, v, position(0) <= position(1))
    o_ref[...] = out
    lse_ref[pl.ds(head, 1), :] = lse


def far_kernel(at_half, heads, where_ref, q_ref, *refs):
    *kv_refs, o_ref, lse_ref = refs
    count = len(kv_refs) // 2
    k_refs, v_refs = kv_refs[:count], kv_refs[count:]
    head = pl.program_id(0)

    @pl.when(where_ref[1] == at_half)
    def _():
        k, v = (jnp.concatenate([r[...] for r in part], axis=0) for part in (k_refs, v_refs))
        out, lse = softmax_part(q_ref[...], k, v, None)
        o_ref[pl.ds(pl.multiple_of(head * HD, HD), HD), :] = out
        lse_ref[pl.ds(head, 1), :] = lse

        @pl.when(head == heads - 1)
        def _():
            rest = lse_ref[0:heads, :]
            terms = []
            for _ in range(3):
                term = rest.astype(jnp.bfloat16).astype(jnp.float32)
                terms.append(term)
                rest = rest - term
            terms.append(jnp.zeros((16 - 3 * heads, SEQ_HALF), jnp.float32))
            o_ref[pl.ds(heads * HD, 16), :] = jnp.concatenate(terms, axis=0).astype(jnp.bfloat16)


def attention_cost(heads):
    return pl.CostEstimate(
        flops=heads * 4 * SEQ_HALF * SEQ_HALF * HD, bytes_accessed=2 * 1024 * 1024,
        transcendentals=heads * SEQ_HALF * SEQ_HALF)


def attend_own(where, chunk, q, kv):
    heads = GROUP // HD
    q_spec = pl.BlockSpec((ROWS, HD), lambda h, w: (0, heads * chunk + h))
    k_spec = pl.BlockSpec((ROWS, HD), lambda h, w: (0, h))
    v_spec = pl.BlockSpec((ROWS, HD), lambda h, w: (0, heads + h))
    return pl.pallas_call(
        own_kernel,
        grid_spec=pltpu.PrefetchScalarGridSpec(
            num_scalar_prefetch=1,
            grid=(heads,),
            in_specs=[q_spec] * 4 + [k_spec] * 4 + [v_spec] * 4,
            out_specs=[
                pl.BlockSpec((HD, SEQ_HALF), lambda h, w: (h, 0)),
                pl.BlockSpec((8, SEQ_HALF), lambda h, w: (0, 0)),
            ],
        ),
        out_shape=[
            jax.ShapeDtypeStruct((GROUP, SEQ_HALF), jnp.bfloat16),
            jax.ShapeDtypeStruct((8, SEQ_HALF), jnp.float32),
        ],
        compiler_params=pltpu.CompilerParams(vmem_limit_bytes=24 * 1024 * 1024),
        cost_estimate=attention_cost(heads),
        name="attend_own",
    )(where, *q, *kv, *kv)


def attend_far(where, at_half, q, kv, k_at, v_at):
    count = len(kv)
    heads = q.shape[1] // HD
    q_spec = pl.BlockSpec((SEQ_HALF, HD), lambda h, w: (0, h))
    k_spec = pl.BlockSpec((SEQ_HALF // count, HD), lambda h, w: (0, k_at + h))
    v_spec = pl.BlockSpec((SEQ_HALF // count, HD), lambda h, w: (0, v_at + h))
    return pl.pallas_call(
        functools.partial(far_kernel, at_half, heads),
        grid_spec=pltpu.PrefetchScalarGridSpec(
            num_scalar_prefetch=1,
            grid=(heads,),
            in_specs=[q_spec] + [k_spec] * count + [v_spec] * count,
            out_specs=pl.BlockSpec((heads * HD + 16, SEQ_HALF), lambda h, w: (0, 0)),
            scratch_shapes=[pltpu.VMEM((8, SEQ_HALF), jnp.float32)],
        ),
        out_shape=jax.ShapeDtypeStruct((heads * HD + 16, SEQ_HALF), jnp.bfloat16),
        compiler_params=pltpu.CompilerParams(vmem_limit_bytes=24 * 1024 * 1024),
        cost_estimate=attention_cost(heads),
        name="attend_far",
    )(where, q, *kv, *kv)


def merge_kernel(where_ref, own_ref, *refs):
    *far_refs, own_lse_ref, out_ref = refs
    late = where_ref[1] == 1
    at = 0
    for far_ref in far_refs:
        heads = far_ref.shape[0] // HD
        terms = far_ref[pl.ds(heads * HD, 16), :].astype(jnp.float32)
        far_lse = terms[0:heads] + terms[heads : 2 * heads] + terms[2 * heads : 3 * heads]
        far_lse = jnp.where(late, far_lse, -1e30)
        own_lse = own_lse_ref[at : at + heads, :]
        highest = jnp.maximum(own_lse, far_lse)
        own_part = jnp.exp2(own_lse - highest)
        far_part = jnp.exp2(far_lse - highest)
        total = own_part + far_part
        own_part = own_part / total
        far_part = far_part / total
        for head in range(heads):
            rows = pl.ds((at + head) * HD, HD)
            mixed = own_ref[rows, :].astype(jnp.float32) * own_part[head : head + 1]
            far = jnp.where(late, far_ref[pl.ds(head * HD, HD), :].astype(jnp.float32), 0.0)
            mixed = mixed + far * far_part[head : head + 1]
            out_ref[:, rows] = mixed.T.astype(jnp.bfloat16)
        at += heads


def merge(where, own, far, own_lse):
    whole = pl.BlockSpec(memory_space=pltpu.VMEM)
    return pl.pallas_call(
        merge_kernel,
        in_specs=[pl.BlockSpec(memory_space=pltpu.SMEM)] + [whole] * (len(far) + 2),
        out_specs=whole,
        out_shape=jax.ShapeDtypeStruct((SEQ_HALF, GROUP), jnp.bfloat16),
        compiler_params=pltpu.CompilerParams(vmem_limit_bytes=16 * 1024 * 1024),
        cost_estimate=pl.CostEstimate(flops=4 * 512 * 512, bytes_accessed=3 * 512 * 1024, transcendentals=0),
        name="merge_halves",
    )(where, own, *far, own_lse)


def norm_kernel(where_ref, *refs):
    own_refs, peer_refs = refs[0:2], refs[2:4]
    res_ref, gain_ref, bias_ref, out_ref = refs[4:8]
    core, x = where_ref[2], where_ref[3]
    blocks = []
    for half, parts in ((core, own_refs), (1 - core, peer_refs)):
        for apart, part, column in ((0, 0, 0), (-1, 0, 1), (1, 1, 0), (2, 1, 1)):
            at = ((x + apart) & 3) * (2 * BLOCK) + half * BLOCK
            at = pl.ds(pl.multiple_of(at, 128), BLOCK)
            added = parts[part][:, pl.ds(column * BLOCK, BLOCK)].astype(jnp.float32)
            blocks.append((at, deepnorm_alpha * res_ref[:, at].astype(jnp.float32) + added))
    mean = sum(jnp.sum(b, -1, keepdims=True) for _, b in blocks) / D
    blocks = [(at, b - mean) for at, b in blocks]
    var = sum(jnp.sum(b * b, -1, keepdims=True) for _, b in blocks) / D
    inv = lax.rsqrt(var + norm_eps)
    for at, b in blocks:
        out_ref[:, at] = (b * inv * gain_ref[:, at] + bias_ref[:, at]).astype(jnp.bfloat16)


def layer_norm(where, own, peer, residual, gain, bias):
    rows = 32
    part = pl.BlockSpec((rows, 2 * BLOCK), lambda i, w: (i, 0))
    full = pl.BlockSpec((rows, D), lambda i, w: (i, 0))
    vector = pl.BlockSpec((1, D), lambda i, w: (0, 0))
    return pl.pallas_call(
        norm_kernel,
        grid_spec=pltpu.PrefetchScalarGridSpec(
            num_scalar_prefetch=1,
            grid=(ROWS // rows,),
            in_specs=[part] * 4 + [full, vector, vector],
            out_specs=full,
        ),
        out_shape=jax.ShapeDtypeStruct((ROWS, D), jnp.bfloat16),
        compiler_params=pltpu.CompilerParams(vmem_limit_bytes=24 * 1024 * 1024),
        cost_estimate=pl.CostEstimate(flops=10 * ROWS * D, bytes_accessed=6 * ROWS * D, transcendentals=0),
        name="layer_norm",
    )(where, *own, *peer, residual, gain.reshape(1, D), bias.reshape(1, D))


def after(value, *others):
    return lax.optimization_barrier((value, *others))[0]


def columns_for(arrays, y, starts):
    return [
        jnp.concatenate(
            [lax.dynamic_slice_in_dim(a, s + ((y + step) & 3) * GROUP, GROUP, axis=1) for a, s in zip(arrays, starts)],
            axis=1,
        )
        for step in range(4)
    ]


def forward(part, step):
    return lax.ppermute(part, "y", ring(4, step))


def put(column, part, at):
    return lax.dynamic_update_slice(column, part[None], (at & 7, 0, 0))


def send(block, step):
    return lax.ppermute(block.astype(jnp.bfloat16), "y", ring(4, step))


def local(queries, keys, values, residual_in, out_weight, norm_gain, norm_bias):
    y = lax.axis_index("y")
    zh = lax.axis_index("zh")
    core = lax.axis_index("c")
    where = jnp.stack([y, zh, core, lax.axis_index("x")]).astype(jnp.int32)

    z = zh * 4 + lax.axis_index("zl")
    up_z = functools.partial(lax.ppermute, axis_name=("zl", "zh"), perm=z_ring(1))
    down_z = functools.partial(lax.ppermute, axis_name=("zl", "zh"), perm=z_ring(-1))

    shard = out_weight.T
    up = [shard, up_z(shard)]
    down = [shard, down_z(shard)]
    q = columns_for([queries, queries], y, [0, 2048])
    q = [q[0]] + [forward(q[s], s) for s in (1, 2, 3)]
    up.append(up_z(up[1]))
    down.append(down_z(down[1]))

    up[2], down[2], keys, values, *_ = lax.optimization_barrier((up[2], down[2], keys, values, *q))
    up.append(up_z(up[2]))
    down.append(down_z(down[2]))
    kv_1 = columns_for([keys, values], y, [2048, 2048])
    kv_1 = [kv_1[0]] + [forward(kv_1[s], s) for s in (1, 2, 3)]
    up.append(up_z(up[3]))

    q_first, q_next, q_last = (
        jnp.concatenate([b[:, start:end] for b in q], axis=0) for start, end in ((0, 512), (512, 768), (768, 1024))
    )
    last_kv = jnp.concatenate(
        [jnp.concatenate([b[:, at : at + PAIR] for b in kv_1], axis=0) for at in (PAIR, 3 * PAIR)], axis=1
    )
    q_first, last_kv, keys, values, *_ = lax.optimization_barrier(
        (q_first, last_kv, keys, values, up[4], down[3], *kv_1)
    )
    q_first = lax.ppermute(q_first, "zh", [(1, 0)])
    far_kv = lax.ppermute(last_kv, "zh", [(0, 1)])
    kv_0 = columns_for([keys, values], y, [0, 0])
    kv_0 = [kv_0[0]] + [forward(kv_0[s], s) for s in (1, 2, 3)]

    q_next = lax.ppermute(after(q_next, kv_0[1], kv_0[3]), "zh", [(1, 0)])

    weight = jnp.zeros((8, 224, GROUP), jnp.bfloat16)
    for step in range(5):
        weight = put(weight, up[step], z - step)
        if 0 < step < 4:
            weight = put(weight, down[step], z + step)
    weight = weight.reshape(2, 2, 2, 224, GROUP)
    mine = lax.dynamic_index_in_dim(weight, core, 1, keepdims=False)
    theirs = lax.ppermute(lax.dynamic_index_in_dim(weight, 1 - core, 1, keepdims=False), "c", ring(2, 1))
    first = jnp.where(core == 0, mine, theirs)
    second = jnp.where(core == 0, theirs, mine)
    weight = jnp.stack([first, second], axis=2).reshape(2, BLOCK, GROUP)
    left = lax.ppermute(weight, "x", ring(4, 1))
    right = lax.ppermute(weight, "x", ring(4, -1))

    far_first = attend_far(where, 0, after(q_first, weight), kv_0, 0, 4)
    q[0] = after(q[0], far_first)
    far_first = lax.ppermute(after(far_first, far_kv), "zh", [(0, 1)])
    far_last = attend_far(where, 1, q_last, [far_kv], 0, 2)
    own_0, lse_0 = attend_own(where, 0, q, kv_0)
    own_1, lse_1 = attend_own(where, 1, q, kv_1)
    far_next = attend_far(where, 0, after(q_next, own_0, own_1, far_last), kv_1, 0, 4)
    far_first = after(far_first, far_next)
    far_next = lax.ppermute(far_next, "zh", [(0, 1)])
    out_0 = merge(where, after(own_0, left, right), [far_first], lse_0)
    out_1 = merge(where, after(own_1, out_0), [far_next, far_last], lse_1)
    outs = [out_0, out_1]
    peers = [lax.ppermute(out, "c", ring(2, 1)) for out in outs]
    own, other = (
        [jnp.concatenate([part[s * ROWS : (s + 1) * ROWS] for part in parts], axis=1) for s in range(4)]
        for parts in (outs, peers)
    )

    *heads, _ = lax.optimization_barrier((*own, *other, peers[1]))
    own, other = heads[:4], heads[4:]
    far = jnp.stack([lax.ppermute(left[0], "x", ring(4, 1)), lax.ppermute(right[1], "x", ring(4, -1))])
    weights = [jnp.concatenate([weight, left], axis=1), jnp.concatenate([right, far], axis=1)]

    sums = []
    peer_sums = []
    for weight in weights:

        def project(heads):
            return lax.dot_general(
                heads.reshape(ROWS, 2, GROUP), weight, (((1, 2), (0, 2)), ((), ())),
                preferred_element_type=jnp.float32,
            )

        up_1 = send(project(own[2]), 1)
        down_1 = send(project(other[2]), -1)
        up_2 = send(project(other[3]), 1)
        down_2 = send(project(own[1]), -1)
        up_3 = send(project(own[3]) + up_1.astype(jnp.float32), 1)
        down_3 = send(project(other[1]) + down_1.astype(jnp.float32), -1)
        total_other = project(other[0]) + up_2.astype(jnp.float32) + down_3.astype(jnp.float32)
        peer_sums.append(lax.ppermute(total_other.astype(jnp.bfloat16), "c", ring(2, 1)))
        total_own = project(own[0]) + down_2.astype(jnp.float32) + up_3.astype(jnp.float32)
        sums.append(total_own.astype(jnp.bfloat16))
        own[2], other[2], _, _ = lax.optimization_barrier((own[2], other[2], up_2, down_2))
        own[1], other[3], _, _ = lax.optimization_barrier((own[1], other[3], up_3, down_3))
    return layer_norm(where, sums, peer_sums, residual_in, norm_gain, norm_bias)


def solution(mesh):
    fine = Mesh(mesh.devices.reshape(4, 4, 2, 2, 4), AXES)
    tokens = P(AXES, None)
    in_specs = (tokens, tokens, tokens, tokens, P(("zh", "y"), ("x", "zl", "c")), P(), P())
    return jax.shard_map(local, mesh=fine, in_specs=in_specs, out_specs=tokens, check_vma=False)
```

```python
import functools
import math

import jax
import jax.numpy as jnp
from jax import lax
from jax.experimental import pallas as pl
from jax.experimental.pallas import tpu as pltpu
from jax.sharding import Mesh, PartitionSpec as P

HD = 128
GROUP = 512
ROWS = 128
SEQ_HALF = 512
PAIR = 2 * HD
D = 7168
HALF = D // 2
BLOCK = HALF // 4

deepnorm_alpha = 96.0**0.25
norm_eps = 1e-05
score_scale = math.log2(math.e) / math.sqrt(HD)

AXES = ("x", "zl", "c", "zh", "y")


def ring(n, step):
    return [(i, (i + step) % n) for i in range(n)]


def z_ring(step):
    pairs = []
    for z in range(8):
        to = (z + step) % 8
        pairs.append(((z % 4) * 2 + z // 4, (to % 4) * 2 + to // 4))
    return pairs


def softmax_part(q, k, v, keep):
    scores = lax.dot_general(k, q, (((1,), (1,)), ((), ())), preferred_element_type=jnp.float32)
    if keep is not None:
        scores = jnp.where(keep, scores, -1e30)
    highest = jnp.max(scores, axis=0, keepdims=True)
    expo = jnp.exp2((scores - highest) * score_scale)
    total = jnp.sum(expo, axis=0, keepdims=True)
    out = lax.dot_general(
        v, expo.astype(jnp.bfloat16), (((0,), (0,)), ((), ())), preferred_element_type=jnp.float32
    )
    return (out / total).astype(jnp.bfloat16), highest * score_scale + jnp.log2(total)


def own_kernel(where_ref, *refs):
    q_refs, k_refs, v_refs, o_ref, lse_ref = refs[0:4], refs[4:8], refs[8:12], refs[12], refs[13]
    head = pl.program_id(0)
    y = where_ref[0]
    q, k, v = (jnp.concatenate([r[...] for r in part], axis=0) for part in (q_refs, k_refs, v_refs))

    def position(axis):
        at = lax.broadcasted_iota(jnp.int32, (SEQ_HALF, SEQ_HALF), axis)
        return ((y - at // ROWS) & 3) * ROWS + (at & (ROWS - 1))

    out, lse = softmax_part(q, k, v, position(0) <= position(1))
    o_ref[...] = out
    lse_ref[pl.ds(head, 1), :] = lse


def far_kernel(at_half, heads, where_ref, q_ref, *refs):
    *kv_refs, o_ref, lse_ref = refs
    count = len(kv_refs) // 2
    k_refs, v_refs = kv_refs[:count], kv_refs[count:]
    head = pl.program_id(0)

    @pl.when(where_ref[1] == at_half)
    def _():
        k, v = (jnp.concatenate([r[...] for r in part], axis=0) for part in (k_refs, v_refs))
        out, lse = softmax_part(q_ref[...], k, v, None)
        o_ref[pl.ds(pl.multiple_of(head * HD, HD), HD), :] = out
        lse_ref[pl.ds(head, 1), :] = lse

        @pl.when(head == heads - 1)
        def _():
            rest = lse_ref[0:heads, :]
            terms = []
            for _ in range(3):
                term = rest.astype(jnp.bfloat16).astype(jnp.float32)
                terms.append(term)
                rest = rest - term
            terms.append(jnp.zeros((16 - 3 * heads, SEQ_HALF), jnp.float32))
            o_ref[pl.ds(heads * HD, 16), :] = jnp.concatenate(terms, axis=0).astype(jnp.bfloat16)


def attention_cost(heads):
    return pl.CostEstimate(
        flops=heads * 4 * SEQ_HALF * SEQ_HALF * HD, bytes_accessed=2 * 1024 * 1024,
        transcendentals=heads * SEQ_HALF * SEQ_HALF)


def attend_own(where, chunk, q, kv):
    heads = GROUP // HD
    q_spec = pl.BlockSpec((ROWS, HD), lambda h, w: (0, heads * chunk + h))
    k_spec = pl.BlockSpec((ROWS, HD), lambda h, w: (0, h))
    v_spec = pl.BlockSpec((ROWS, HD), lambda h, w: (0, heads + h))
    return pl.pallas_call(
        own_kernel,
        grid_spec=pltpu.PrefetchScalarGridSpec(
            num_scalar_prefetch=1,
            grid=(heads,),
            in_specs=[q_spec] * 4 + [k_spec] * 4 + [v_spec] * 4,
            out_specs=[
                pl.BlockSpec((HD, SEQ_HALF), lambda h, w: (h, 0)),
                pl.BlockSpec((8, SEQ_HALF), lambda h, w: (0, 0)),
            ],
        ),
        out_shape=[
            jax.ShapeDtypeStruct((GROUP, SEQ_HALF), jnp.bfloat16),
            jax.ShapeDtypeStruct((8, SEQ_HALF), jnp.float32),
        ],
        compiler_params=pltpu.CompilerParams(vmem_limit_bytes=24 * 1024 * 1024),
        cost_estimate=attention_cost(heads),
        name="attend_own",
    )(where, *q, *kv, *kv)


def attend_far(where, at_half, q, kv, k_at, v_at):
    count = len(kv)
    heads = q.shape[1] // HD
    q_spec = pl.BlockSpec((SEQ_HALF, HD), lambda h, w: (0, h))
    k_spec = pl.BlockSpec((SEQ_HALF // count, HD), lambda h, w: (0, k_at + h))
    v_spec = pl.BlockSpec((SEQ_HALF // count, HD), lambda h, w: (0, v_at + h))
    return pl.pallas_call(
        functools.partial(far_kernel, at_half, heads),
        grid_spec=pltpu.PrefetchScalarGridSpec(
            num_scalar_prefetch=1,
            grid=(heads,),
            in_specs=[q_spec] + [k_spec] * count + [v_spec] * count,
            out_specs=pl.BlockSpec((heads * HD + 16, SEQ_HALF), lambda h, w: (0, 0)),
            scratch_shapes=[pltpu.VMEM((8, SEQ_HALF), jnp.float32)],
        ),
        out_shape=jax.ShapeDtypeStruct((heads * HD + 16, SEQ_HALF), jnp.bfloat16),
        compiler_params=pltpu.CompilerParams(vmem_limit_bytes=24 * 1024 * 1024),
        cost_estimate=attention_cost(heads),
        name="attend_far",
    )(where, q, *kv, *kv)


def merge_kernel(where_ref, own_ref, *refs):
    *far_refs, own_lse_ref, out_ref = refs
    late = where_ref[1] == 1
    at = 0
    for far_ref in far_refs:
        heads = far_ref.shape[0] // HD
        terms = far_ref[pl.ds(heads * HD, 16), :].astype(jnp.float32)
        far_lse = terms[0:heads] + terms[heads : 2 * heads] + terms[2 * heads : 3 * heads]
        far_lse = jnp.where(late, far_lse, -1e30)
        own_lse = own_lse_ref[at : at + heads, :]
        highest = jnp.maximum(own_lse, far_lse)
        own_part = jnp.exp2(own_lse - highest)
        far_part = jnp.exp2(far_lse - highest)
        total = own_part + far_part
        own_part = own_part / total
        far_part = far_part / total
        for head in range(heads):
            rows = pl.ds((at + head) * HD, HD)
            mixed = own_ref[rows, :].astype(jnp.float32) * own_part[head : head + 1]
            far = jnp.where(late, far_ref[pl.ds(head * HD, HD), :].astype(jnp.float32), 0.0)
            mixed = mixed + far * far_part[head : head + 1]
            out_ref[:, rows] = mixed.T.astype(jnp.bfloat16)
        at += heads


def merge(where, own, far, own_lse):
    whole = pl.BlockSpec(memory_space=pltpu.VMEM)
    return pl.pallas_call(
        merge_kernel,
        in_specs=[pl.BlockSpec(memory_space=pltpu.SMEM)] + [whole] * (len(far) + 2),
        out_specs=whole,
        out_shape=jax.ShapeDtypeStruct((SEQ_HALF, GROUP), jnp.bfloat16),
        compiler_params=pltpu.CompilerParams(vmem_limit_bytes=16 * 1024 * 1024),
        cost_estimate=pl.CostEstimate(flops=4 * 512 * 512, bytes_accessed=3 * 512 * 1024, transcendentals=0),
        name="merge_halves",
    )(where, own, *far, own_lse)


def norm_kernel(where_ref, *refs):
    own_refs, peer_refs = refs[0:2], refs[2:4]
    res_ref, gain_ref, bias_ref, out_ref = refs[4:8]
    core, x = where_ref[2], where_ref[3]
    blocks = []
    for half, parts in ((core, own_refs), (1 - core, peer_refs)):
        for apart, part, column in ((0, 0, 0), (-1, 0, 1), (1, 1, 0), (2, 1, 1)):
            at = ((x + apart) & 3) * (2 * BLOCK) + half * BLOCK
            at = pl.ds(pl.multiple_of(at, 128), BLOCK)
            added = parts[part][:, pl.ds(column * BLOCK, BLOCK)].astype(jnp.float32)
            blocks.append((at, deepnorm_alpha * res_ref[:, at].astype(jnp.float32) + added))
    mean = sum(jnp.sum(b, -1, keepdims=True) for _, b in blocks) / D
    blocks = [(at, b - mean) for at, b in blocks]
    var = sum(jnp.sum(b * b, -1, keepdims=True) for _, b in blocks) / D
    inv = lax.rsqrt(var + norm_eps)
    for at, b in blocks:
        out_ref[:, at] = (b * inv * gain_ref[:, at] + bias_ref[:, at]).astype(jnp.bfloat16)


def layer_norm(where, own, peer, residual, gain, bias):
    rows = 32
    part = pl.BlockSpec((rows, 2 * BLOCK), lambda i, w: (i, 0))
    full = pl.BlockSpec((rows, D), lambda i, w: (i, 0))
    vector = pl.BlockSpec((1, D), lambda i, w: (0, 0))
    return pl.pallas_call(
        norm_kernel,
        grid_spec=pltpu.PrefetchScalarGridSpec(
            num_scalar_prefetch=1,
            grid=(ROWS // rows,),
            in_specs=[part] * 4 + [full, vector, vector],
            out_specs=full,
        ),
        out_shape=jax.ShapeDtypeStruct((ROWS, D), jnp.bfloat16),
        compiler_params=pltpu.CompilerParams(vmem_limit_bytes=24 * 1024 * 1024),
        cost_estimate=pl.CostEstimate(flops=10 * ROWS * D, bytes_accessed=6 * ROWS * D, transcendentals=0),
        name="layer_norm",
    )(where, *own, *peer, residual, gain.reshape(1, D), bias.reshape(1, D))


def after(value, *others):
    return lax.optimization_barrier((value, *others))[0]


def columns_for(arrays, y, starts):
    return [
        jnp.concatenate(
            [lax.dynamic_slice_in_dim(a, s + ((y + step) & 3) * GROUP, GROUP, axis=1) for a, s in zip(arrays, starts)],
            axis=1,
        )
        for step in range(4)
    ]


def forward(part, step):
    return lax.ppermute(part, "y", ring(4, step))


def put(column, part, at):
    return lax.dynamic_update_slice(column, part[None], (at & 7, 0, 0))


def send(block, step):
    return lax.ppermute(block.astype(jnp.bfloat16), "y", ring(4, step))


def local(queries, keys, values, residual_in, out_weight, norm_gain, norm_bias):
    y = lax.axis_index("y")
    zh = lax.axis_index("zh")
    core = lax.axis_index("c")
    where = jnp.stack([y, zh, core, lax.axis_index("x")]).astype(jnp.int32)

    z = zh * 4 + lax.axis_index("zl")
    up_z = functools.partial(lax.ppermute, axis_name=("zl", "zh"), perm=z_ring(1))
    down_z = functools.partial(lax.ppermute, axis_name=("zl", "zh"), perm=z_ring(-1))

    shard = out_weight.T
    up = [shard, up_z(shard)]
    down = [shard, down_z(shard)]
    q = columns_for([queries, queries], y, [0, 2048])
    q = [q[0]] + [forward(q[s], s) for s in (1, 2, 3)]
    up.append(up_z(up[1]))
    down.append(down_z(down[1]))

    up[2], down[2], keys, values, *_ = lax.optimization_barrier((up[2], down[2], keys, values, *q))
    up.append(up_z(up[2]))
    down.append(down_z(down[2]))
    kv_1 = columns_for([keys, values], y, [2048, 2048])
    kv_1 = [kv_1[0]] + [forward(kv_1[s], s) for s in (1, 2, 3)]
    up.append(up_z(up[3]))

    q_first, q_next, q_last = (
        jnp.concatenate([b[:, start:end] for b in q], axis=0) for start, end in ((0, 512), (512, 768), (768, 1024))
    )
    last_kv = jnp.concatenate(
        [jnp.concatenate([b[:, at : at + PAIR] for b in kv_1], axis=0) for at in (PAIR, 3 * PAIR)], axis=1
    )
    q_first, last_kv, keys, values, *_ = lax.optimization_barrier(
        (q_first, last_kv, keys, values, up[4], down[3], *kv_1)
    )
    q_first = lax.ppermute(q_first, "zh", [(1, 0)])
    far_kv = lax.ppermute(last_kv, "zh", [(0, 1)])
    kv_0 = columns_for([keys, values], y, [0, 0])
    kv_0 = [kv_0[0]] + [forward(kv_0[s], s) for s in (1, 2, 3)]

    q_next = lax.ppermute(after(q_next, kv_0[1], kv_0[3]), "zh", [(1, 0)])

    weight = jnp.zeros((8, 224, GROUP), jnp.bfloat16)
    for step in range(5):
        weight = put(weight, up[step], z - step)
        if 0 < step < 4:
            weight = put(weight, down[step], z + step)
    weight = weight.reshape(2, 2, 2, 224, GROUP)
    mine = lax.dynamic_index_in_dim(weight, core, 1, keepdims=False)
    theirs = lax.ppermute(lax.dynamic_index_in_dim(weight, 1 - core, 1, keepdims=False), "c", ring(2, 1))
    first = jnp.where(core == 0, mine, theirs)
    second = jnp.where(core == 0, theirs, mine)
    weight = jnp.stack([first, second], axis=2).reshape(2, BLOCK, GROUP)
    left = lax.ppermute(weight, "x", ring(4, 1))
    right = lax.ppermute(weight, "x", ring(4, -1))

    far_first = attend_far(where, 0, after(q_first, weight), kv_0, 0, 4)
    q[0] = after(q[0], far_first)
    far_first = lax.ppermute(after(far_first, far_kv), "zh", [(0, 1)])
    far_last = attend_far(where, 1, q_last, [far_kv], 0, 2)
    own_0, lse_0 = attend_own(where, 0, q, kv_0)
    own_1, lse_1 = attend_own(where, 1, q, kv_1)
    left, right, q_next, *_ = lax.optimization_barrier((left, right, q_next, own_0, own_1, far_last))
    far_next = attend_far(where, 0, q_next, kv_1, 0, 4)
    far = jnp.stack([lax.ppermute(left[0], "x", ring(4, 1)), lax.ppermute(right[1], "x", ring(4, -1))])
    far_first = after(far_first, far_next)
    far_next = lax.ppermute(far_next, "zh", [(0, 1)])
    out_0 = merge(where, own_0, [far_first], lse_0)
    out_1 = merge(where, after(own_1, out_0), [far_next, far_last], lse_1)
    outs = [out_0, out_1]
    peers = [lax.ppermute(out, "c", ring(2, 1)) for out in outs]
    own, other = (
        [jnp.concatenate([part[s * ROWS : (s + 1) * ROWS] for part in parts], axis=1) for s in range(4)]
        for parts in (outs, peers)
    )

    *heads, _ = lax.optimization_barrier((*own, *other, peers[1]))
    own, other = heads[:4], heads[4:]
    own[1], other[3], _ = lax.optimization_barrier((own[1], other[3], far))
    weights = [jnp.concatenate([weight, left], axis=1), jnp.concatenate([right, far], axis=1)]

    sums = []
    peer_sums = []
    for weight in weights:

        def project(heads):
            return lax.dot_general(
                heads.reshape(ROWS, 2, GROUP), weight, (((1, 2), (0, 2)), ((), ())),
                preferred_element_type=jnp.float32,
            )

        up_1 = send(project(own[2]), 1)
        down_1 = send(project(other[2]), -1)
        up_2 = send(project(other[3]), 1)
        down_2 = send(project(own[1]), -1)
        up_3 = send(project(own[3]) + up_1.astype(jnp.float32), 1)
        down_3 = send(project(other[1]) + down_1.astype(jnp.float32), -1)
        total_other = project(other[0]) + up_2.astype(jnp.float32) + down_3.astype(jnp.float32)
        peer_sums.append(lax.ppermute(total_other.astype(jnp.bfloat16), "c", ring(2, 1)))
        total_own = project(own[0]) + down_2.astype(jnp.float32) + up_3.astype(jnp.float32)
        sums.append(total_own.astype(jnp.bfloat16))
        own[2], other[2], _, _ = lax.optimization_barrier((own[2], other[2], up_2, down_2))
        own[1], other[3], _, _ = lax.optimization_barrier((own[1], other[3], up_3, down_3))
    return layer_norm(where, sums, peer_sums, residual_in, norm_gain, norm_bias)


def solution(mesh):
    fine = Mesh(mesh.devices.reshape(4, 4, 2, 2, 4), AXES)
    tokens = P(AXES, None)
    in_specs = (tokens, tokens, tokens, tokens, P(("zh", "y"), ("x", "zl", "c")), P(), P())
    return jax.shard_map(local, mesh=fine, in_specs=in_specs, out_specs=tokens, check_vma=False)
```
